32 devices in a mesh: dp: 2 (over z_hi), seq: 8 (over y, x, core), tensor: 2 (over z_lo).
Axes of the slice: x: 2, y: 2, z: 4 (z_hi: 2, z_lo: 2; z = z_hi * 2 + z_lo), core: 2. Of those that a mesh axis runs over, the one named last changes fastest.
Arguments:
- queries: bfloat16 [2, 4096, 4096], P('dp', 'seq', 'tensor'), may hold values from -6 to 6
- keys: bfloat16 [2, 4096, 4096], P('dp', 'seq', 'tensor'), may hold values from -6 to 6
- values: bfloat16 [2, 4096, 4096], P('dp', 'seq', 'tensor'), may hold values from -40 to 40
- grad_out: bfloat16 [2, 4096, 4096], P('dp', 'seq', 'tensor'), may hold values from -48 to 48
- doc_lengths: int32 [2, 4], P('dp'), may hold values from 1 to 3072, 4096 in all within a row
- gain: float32 [4096], P('tensor'), may hold values from 0.1 to 1.9
Outputs:
- layer_out: bfloat16 [2, 4096, 4096], P('dp', 'seq', 'tensor')
- grad_queries: bfloat16 [2, 4096, 4096], P('dp', 'seq', 'tensor')
- grad_keys: bfloat16 [2, 4096, 4096], P('dp', 'seq', 'tensor')
- grad_values: bfloat16 [2, 4096, 4096], P('dp', 'seq', 'tensor')
- grad_gain: float32 [4096], P('tensor')
The draws below stay inside these ranges and needn't reach their ends.
Inputs may be any that keep to these rules, and one draw needn't show every extreme that they name: `doc_lengths`: each row sums to 4096; in every sequence the longest document has exactly 3072 tokens.
All inputs are finite; a program needn't handle non-finite values.
Results may differ from the reference program's by a relative error of at most 0.0063.
Values may be sent and summed in bfloat16 or wider, within the bound.
A program may use at most 128 MiB of HBM per device.

```python
import math
import jax
import jax.numpy as jnp
import numpy as np
from jax import lax

HEADS = 32
HD = 128
TOK_DEV = 512
WIDTH = 4096
SEQS = 2
LENGTH = 4096
DOCS = 4
MOST = 3072
N_SEQ = 8


def draw_values(key, part):
    first, second = jax.random.split(key, 2)
    heads = jnp.arange(HEADS, dtype=jnp.float32)
    jitter = jax.random.uniform(first, (HEADS,), dtype=jnp.float32)
    base = jnp.clip(jax.random.normal(second, (SEQS, LENGTH, HEADS, HD), dtype=jnp.float32), -4.0, 4.0)
    scale = 10.0 ** ((heads + jitter) / HEADS)
    return (base * scale[None, None, :, None]).reshape(SEQS, LENGTH, WIDTH).astype(jnp.bfloat16)


def draw_grad_out(key, part):
    first, second = jax.random.split(key, 2)
    place = jnp.arange(LENGTH, dtype=jnp.float32) / LENGTH
    rows = (3.0 ** place)[None, :] * jnp.exp(jax.random.uniform(first, (SEQS, LENGTH), dtype=jnp.float32, minval=0.0, maxval=1.386))
    base = jnp.clip(jax.random.normal(second, (SEQS, LENGTH, WIDTH), dtype=jnp.float32), -4.0, 4.0)
    return (base * rows[:, :, None]).astype(jnp.bfloat16)


def levels(stream_key, extent, shards, smallest, largest):
    level = 1.0
    for dim, parts in shards:
        heights = jax.random.uniform(jax.random.fold_in(jax.random.fold_in(stream_key, 6), dim), (parts,), jnp.float32, smallest / len(shards), largest / len(shards))
        level = level * jnp.repeat(jnp.exp(heights), extent[dim] // parts).reshape((-1,) + (1,) * (len(extent) - 1 - dim))
    return level


def length_profile(count, total, bound, slope):
    loads = [(1 << 20) // math.isqrt(grade ** slope) + 1 for grade in range(2, count + 1)]
    rest, counts = total - bound - (count - 1), [1] * (count - 1)
    while rest > 0:
        candidates = [i for i in range(count - 1) if counts[i] < bound]
        pool, left = sum([loads[i] for i in candidates]), rest
        for i in candidates:
            more = min(bound - counts[i], max(1, left * loads[i] // pool), rest)
            counts[i] = counts[i] + more
            rest = rest - more
    return np.array([bound] + counts)


def uneven(key, number_of, total, limit, skew):
    if number_of == 2:
        one = jax.random.randint(key, (), max(1, total - limit), min(limit, total - 1) + 1)
        return jnp.stack([one, total - one])
    sizes = jnp.asarray(length_profile(number_of, total, limit, skew), jnp.int32)
    twos = (number_of - 1) // 2
    donor, sink = sizes[1:1 + 2 * twos:2], sizes[2:2 + 2 * twos:2]
    slack = jnp.minimum(donor - 1, limit - sink)
    moved = jax.random.randint(jax.random.fold_in(key, 1), (twos,), 0, 1 << 20) % (slack + 1)
    sizes = sizes.at[1:1 + 2 * twos:2].set(donor - moved).at[2:2 + 2 * twos:2].set(sink + moved)
    return sizes[jax.random.permutation(jax.random.fold_in(key, 2), number_of)]


def scatter_about(rng, dims, width, bound, cuts=(), held_as=jnp.bfloat16):
    drawn = jax.random.normal(rng, dims, jnp.float32) * width
    if len(cuts) > 0:
        drawn = levels(rng, dims, cuts, -0.22, 0.18) * drawn
    return jnp.clip(drawn, min=-bound, max=bound).astype(held_as)


def setup_inputs(seed: int = 0) -> dict:
    key_list = jax.random.split(jax.random.key(seed), 7)
    queries = scatter_about(key_list[0], (SEQS, LENGTH, WIDTH), 1.0, 6.0, ((0, 2), (1, 8), (2, 2)))
    keys = scatter_about(key_list[1], (SEQS, LENGTH, WIDTH), 1.0, 6.0, ((0, 2), (1, 8), (2, 2)))
    values = draw_values(jax.random.fold_in(key_list[6], 71), 0)
    grad_out = draw_grad_out(jax.random.fold_in(key_list[6], 71), 0)
    doc_lengths = jax.vmap(lambda own: uneven(own, DOCS, LENGTH, MOST, 2))(jax.random.split(key_list[4], SEQS)).reshape((SEQS, DOCS)).astype(jnp.int32)
    gain = jnp.clip(1.0 + 0.18 * jax.random.normal(key_list[5], (WIDTH,), jnp.float32), 0.1, 1.9)
    return {"queries": queries, "keys": keys, "values": values, "grad_out": grad_out, "doc_lengths": doc_lengths, "gain": gain}


epsilon = 1e-05

def block_tables(lengths):
    starts = jnp.cumsum(lengths) - lengths
    position = jnp.arange(LENGTH, dtype=jnp.int32)
    document = lax.optimization_barrier(jnp.sum((starts[None, :] <= position[:, None]).astype(jnp.int32), axis=1)) - 1
    numbers = jnp.arange(N_SEQ, dtype=jnp.int32)
    begins = numbers * TOK_DEV
    continues = jnp.logical_not(jnp.any(starts[None, :] == begins[:, None], axis=1))
    grouped = document.reshape(N_SEQ, TOK_DEV)
    first_doc = grouped[:, 0]
    last_doc = grouped[:, -1]
    first_block = starts[first_doc] // TOK_DEV
    last_block = (starts[last_doc] + lengths[last_doc] - 1) // TOK_DEV
    weight_in = continues[:, None] & (numbers[None, :] >= first_block[:, None]) & (numbers[None, :] < numbers[:, None])
    weight_back = (numbers[None, :] > numbers[:, None]) & (numbers[None, :] <= last_block[:, None])
    first_mask = (grouped == first_doc[:, None]) & continues[:, None]
    last_mask = grouped == last_doc[:, None]
    return (grouped, weight_in, weight_back, first_mask, last_mask)

def causal_scores(left, right, document):
    count = document.shape[0]
    lower = jnp.arange(count)[:, None] >= jnp.arange(count)[None, :]
    same = lower & (document[:, None] == document[None, :])
    raw = jnp.einsum('thd,shd->hts', left.astype(jnp.float32), right.astype(jnp.float32))
    return jnp.where(same[None], raw, 0.0).astype(jnp.bfloat16)

def carry_sum(weights, states):
    total = jnp.einsum('bc,chde->bhde', weights.astype(jnp.float32), states.astype(jnp.float32), precision=lax.Precision.HIGHEST)
    return total.astype(jnp.bfloat16)

def one_sequence(queries, keys, values, grad_out, lengths, gain):
    grouped, weight_in, weight_back, first_mask, last_mask = block_tables(lengths)
    shape = (N_SEQ, TOK_DEV, HEADS, HD)
    query = queries.reshape(shape)
    key = keys.reshape(shape)
    value = values.reshape(shape)
    key_last = jnp.where(last_mask[:, :, None, None], key, 0)
    value_last = jnp.where(last_mask[:, :, None, None], value, 0)
    query_first = jnp.where(first_mask[:, :, None, None], query, 0)
    state = jnp.einsum('bthd,bthe->bhde', key_last.astype(jnp.float32), value.astype(jnp.float32)).astype(jnp.bfloat16)
    carry_in = carry_sum(weight_in, state)

    def forward_block(items):
        query_block, key_block, value_block, doc_block, first_block, carry_block = items
        scores = causal_scores(query_block, key_block, doc_block)
        local = jnp.einsum('hts,shd->thd', scores.astype(jnp.float32), value_block.astype(jnp.float32))
        return local + jnp.einsum('thd,hde->the', first_block.astype(jnp.float32), carry_block.astype(jnp.float32))
    attended = lax.map(forward_block, (query, key, value, grouped, query_first, carry_in)).reshape(LENGTH, WIDTH)
    mean_squares = lax.optimization_barrier(jnp.mean(attended * attended, axis=1))
    rscale = lax.rsqrt(mean_squares + epsilon)
    unit = attended * rscale[:, None]
    layer_out = (gain * unit).astype(jnp.bfloat16)
    upstream = grad_out.astype(jnp.float32)
    gain_term = lax.optimization_barrier(jnp.sum(upstream * unit, axis=0))
    scaled = upstream * gain
    inner = lax.optimization_barrier(jnp.mean(scaled * unit, axis=1))
    d_att = (rscale[:, None] * (scaled - unit * inner[:, None])).astype(jnp.bfloat16).reshape(shape)
    d_first = jnp.where(first_mask[:, :, None, None], d_att, 0)
    back_state = jnp.einsum('bthd,bthe->bhde', query_first.astype(jnp.float32), d_att.astype(jnp.float32)).astype(jnp.bfloat16)
    carry_back = carry_sum(weight_back, back_state)

    def backward_block(items):
        query_block, key_block, value_block, doc_block, grad_block, grad_first, carry_block, value_end, key_end, back_block = items
        scores = causal_scores(query_block, key_block, doc_block)
        d_scores = causal_scores(grad_block, value_block, doc_block)
        grad_query = jnp.einsum('hts,shd->thd', d_scores.astype(jnp.float32), key_block.astype(jnp.float32))
        grad_query = grad_query + jnp.einsum('the,hde->thd', grad_first.astype(jnp.float32), carry_block.astype(jnp.float32))
        grad_key = jnp.einsum('hts,thd->shd', d_scores.astype(jnp.float32), query_block.astype(jnp.float32))
        grad_key = grad_key + jnp.einsum('she,hde->shd', value_end.astype(jnp.float32), back_block.astype(jnp.float32))
        grad_value = jnp.einsum('hts,the->she', scores.astype(jnp.float32), grad_block.astype(jnp.float32))
        grad_value = grad_value + jnp.einsum('shd,hde->she', key_end.astype(jnp.float32), back_block.astype(jnp.float32))
        return (grad_query.astype(jnp.bfloat16), grad_key.astype(jnp.bfloat16), grad_value.astype(jnp.bfloat16))
    grad_query, grad_key, grad_value = lax.map(backward_block, (query, key, value, grouped, d_att, d_first, carry_in, value_last, key_last, carry_back))
    return (layer_out, grad_query.reshape(LENGTH, WIDTH), grad_key.reshape(LENGTH, WIDTH), grad_value.reshape(LENGTH, WIDTH), gain_term)

def reference(queries, keys, values, grad_out, doc_lengths, gain):
    results = [one_sequence(queries[member], keys[member], values[member], grad_out[member], doc_lengths[member], gain) for member in range(SEQS)]
    layer_out = jnp.stack([item[0] for item in results])
    grad_queries = jnp.stack([item[1] for item in results])
    grad_keys = jnp.stack([item[2] for item in results])
    grad_values = jnp.stack([item[3] for item in results])
    grad_gain = results[0][4]
    for item in results[1:]:
        grad_gain = grad_gain + item[4]
    return (layer_out, grad_queries, grad_keys, grad_values, grad_gain)
```

```python
import functools

import jax
import jax.numpy as jnp
from jax import lax
from jax.experimental import pallas as pl
from jax.experimental.pallas import tpu as pltpu
from jax.sharding import PartitionSpec as P

HD = 128
CHUNK = 2
EPSILON = 1e-05
MESH = pl.DeviceIdType.MESH
F32 = jnp.float32
BF16 = jnp.bfloat16


def nn(a, b):
    return lax.dot_general(a, b, (((1,), (0,)), ((), ())), preferred_element_type=F32)


def nt(a, b):
    return lax.dot_general(a, b, (((1,), (1,)), ((), ())), preferred_element_type=F32)


def tn(a, b):
    return lax.dot_general(a, b, (((0,), (0,)), ((), ())), preferred_element_type=F32)


def cols(h):
    return pl.ds(pl.multiple_of(h * HD, HD), HD)


def bits_of(n):
    return n.bit_length() - 1


def kernel(
    sizes, len_ref, q_hbm, k_hbm, v_hbm, g_hbm, gain_ref,
    lo_hbm, gq_hbm, gk_hbm, gv_hbm, gg_ref,
    q, k, v, g, att, gvp, scr, dat, lo, gq, gk, gv, mask, fmf, lmf, fmb, lmb,
    acc, rs, qs, st, sr, sa, rr, pacc, pf, pr, ci, ts, tr, gs, gr,
    in_sem, out_sem, ssem, rsem,
):
    n_dp, n_seq, n_tensor, docs = sizes
    T, W = q.shape
    H = W // HD
    half = H // 2
    C = half // CHUNK
    J = bits_of(n_seq) - 1
    T2 = T // 2
    per = (3 + J) * C
    tensor_base = 2 * per
    gain_base = tensor_base + bits_of(n_tensor)

    loads = [
        pltpu.make_async_copy(src, dst, in_sem.at[i])
        for i, (src, dst) in enumerate(((k_hbm, k), (v_hbm, v), (q_hbm, q), (g_hbm, g)))
    ]
    for load in loads:
        load.start()

    me = lax.axis_index("seq")
    dp = lax.axis_index("dp")
    ten = lax.axis_index("tensor")

    def flip(index, j):
        bit = lax.rem(lax.div(index, 1 << j), 2)
        return index + (1 - 2 * bit) * (1 << j)

    seq_peers = [{"seq": flip(me, j)} for j in range(J + 1)]
    dp_peers = [{"dp": flip(dp, j)} for j in range(bits_of(n_dp))]
    tensor_peers = [{"tensor": flip(ten, j)} for j in range(bits_of(n_tensor))]
    peers = seq_peers + dp_peers + tensor_peers
    barrier = pltpu.get_barrier_semaphore()
    for peer in peers:
        pl.semaphore_signal(barrier, inc=1, device_id=peer, device_id_type=MESH)

    core = lax.rem(me, 2)
    mine = core * half
    other = (1 - core) * half
    begin = me * T

    starts = []
    run = jnp.int32(0)
    for d in range(docs):
        starts.append(run)
        run = run + len_ref[0, d]
    ends = starts[1:] + [run]

    def first_start(pos):
        best = jnp.int32(0)
        for s in starts:
            best = jnp.maximum(best, jnp.where(s <= pos, s, 0))
        return best

    def last_end(pos):
        best = run
        for e in ends:
            best = jnp.minimum(best, jnp.where(e > pos, e, run))
        return best

    def flag(cond):
        return jnp.where(cond, 1.0, 0.0).astype(F32)

    bit_of = [lax.rem(lax.div(me, 1 << j), 2) for j in range(J + 1)]
    fwd, bwd = [], []
    chip = (me - core) * T
    for j in range(J + 1):
        size = 2 << j
        low = lax.div(me, size) * size
        mid = (low + (1 << j)) * T
        high = (low + size) * T
        wf = flag(first_start(high) < mid)
        wb = flag(last_end(low * T - 1) > mid)
        right = flag(bit_of[j] == 1)
        left = 1.0 - right
        fwd.append((
            right + left * wf, left + right * wf,
            right * flag(first_start(chip) < mid),
        ))
        bwd.append((
            left + right * wb, right + left * wb,
            left * flag(last_end(chip + 2 * T - 1) > mid),
        ))
    is_one = flag(core == 1)
    is_zero = 1.0 - is_one
    f_state = is_one * flag(first_start(begin) < begin)
    f_pre = is_zero + is_one * flag(first_start(begin) < chip)
    b_state = is_zero * flag(last_end(begin + T - 1) > begin + T)
    b_pre = is_one + is_zero * flag(last_end(begin + T - 1) > chip + 2 * T)

    row = lax.broadcasted_iota(jnp.int32, (T, HD), 0) + begin
    own_start = first_start(begin)
    keep_first = (row < last_end(begin)) & (own_start < begin)
    keep_last = row >= first_start(begin + T - 1)
    fm = jnp.where(keep_first, 1.0, 0.0).astype(F32)
    lm = jnp.where(keep_last, 1.0, 0.0).astype(F32)
    fmf[...] = fm
    lmf[...] = lm
    fmb[...] = fm.astype(BF16)
    lmb[...] = lm.astype(BF16)
    for r in range(T // HD):
        t_pos = lax.broadcasted_iota(jnp.int32, (HD, T), 0) + (begin + r * HD)
        s_pos = lax.broadcasted_iota(jnp.int32, (HD, T), 1) + begin
        t_start = jnp.zeros((HD, T), jnp.int32)
        for s in starts:
            t_start = jnp.maximum(t_start, jnp.where(t_pos >= s, s, 0))
        inside = (s_pos <= t_pos) & (s_pos >= t_start)
        mask[r * HD:(r + 1) * HD, :] = jnp.where(inside, 1.0, 0.0).astype(F32)

    def remote(src, dst, index, peer):
        return pltpu.make_async_remote_copy(
            src_ref=src, dst_ref=dst, send_sem=ssem.at[index], recv_sem=rsem.at[index],
            device_id=peer, device_id_type=MESH,
        )

    def chunk(c):
        return pl.ds(c * CHUNK, CHUNK)

    def state_copy(w, cc):
        return remote(st.at[w, chunk(cc)], sr.at[w, chunk(cc)], w * per + cc, seq_peers[0])

    def step_copy(w, j, c):
        return remote(
            sa.at[w, j, chunk(c)], rr.at[w, j, chunk(c)],
            w * per + (2 + j) * C + c, seq_peers[j + 1],
        )

    def final_copy(w, c):
        return remote(pf.at[w, chunk(c)], pr.at[w, chunk(c)], w * per + (2 + J) * C + c, seq_peers[0])

    def begin_step(w, coef, c):
        cc = core * C + c
        state_copy(w, cc).wait_recv()
        own, theirs = st[w, chunk(cc)].astype(F32), sr[w, chunk(cc)].astype(F32)
        sa[w, 0, chunk(c)] = (coef[0][0] * own + coef[0][1] * theirs).astype(BF16)
        step_copy(w, 0, c).start()

    def step(w, coef, j, c):
        step_copy(w, j, c).wait_recv()
        got = rr[w, j, chunk(c)].astype(F32)
        keep = coef[j + 1]
        total = keep[2] * got
        if j > 0:
            total = total + pacc[chunk(c)]
        if j < J - 1:
            pacc[chunk(c)] = total
            new = keep[0] * sa[w, j, chunk(c)].astype(F32) + keep[1] * got
            sa[w, j + 1, chunk(c)] = new.astype(BF16)
            step_copy(w, j + 1, c).start()
        else:
            pf[w, chunk(c)] = total.astype(BF16)
            final_copy(w, c).start()

    def interleave(w, coef, work, before, extra):
        order = sorted(
            [(c + j, -j, c) for j in range(J) for c in range(C)]
        )
        events = [functools.partial(begin_step, w, coef, c) for c in range(C)]
        first = len(events)
        events += [functools.partial(step, w, coef, -mj, c) for _, mj, c in order]
        done = 0

        def to(upto):
            nonlocal done
            if upto > done:
                lax.fori_loop(done, upto, lambda h, x: (work(h), x)[1], 0)
                done = upto

        to(before)
        later = len(events) - first
        for i, event in enumerate(events):
            if i >= first:
                to(before + ((H - before) * (i - first + 1)) // later)
            event()
            if extra and i >= first and (i - first) % 2 == 1:
                extra.pop(0)()
        to(H)
        while extra:
            extra.pop(0)()

    loads[0].wait()
    loads[1].wait()
    pl.semaphore_wait(barrier, len(peers))

    def state_chunk(i, x):
        for u in range(CHUNK):
            h = lax.rem(other + i * CHUNK + u, H)
            st[0, h] = tn(k[:, cols(h)] * lmb[...], v[:, cols(h)]).astype(BF16)
        state_copy(0, lax.rem((1 - core) * C + i, 2 * C)).start()
        return x

    lax.fori_loop(0, 2 * C, state_chunk, 0)
    loads[2].wait()

    def local_forward(h):
        qh, kh, vh = q[:, cols(h)], k[:, cols(h)], v[:, cols(h)]
        top = (nt(qh[:T2], kh[:T2]) * mask[:T2, :T2]).astype(BF16)
        low = (nt(qh[T2:], kh) * mask[T2:, :]).astype(BF16)
        scr[h, :T2, :T2] = top
        scr[h, T2:, :] = low
        att[:T2, cols(h)] = nn(top, vh[:T2])
        att[T2:, cols(h)] = nn(low, vh)

    interleave(0, fwd, local_forward, 2, [])
    loads[3].wait()
    acc[...] = jnp.zeros_like(acc)

    def finish_forward(h, pre):
        carry = (f_state * sr[0, h].astype(F32) + f_pre * pre.astype(F32)).astype(BF16)
        ci[h] = carry
        x = att[:, cols(h)] + fmf[...] * nn(q[:, cols(h)], carry)
        att[:, cols(h)] = x
        acc[0] += x * x
        acc[1] += (g[:, cols(h)].astype(F32) * gain_ref[pl.ds(h, 1), :]) * x

    def forward_mine(i, x):
        finish_forward(mine + i, pf[0, i])
        return x

    lax.fori_loop(0, half, forward_mine, 0)

    def forward_other(c, x):
        state_copy(0, (1 - core) * C + c).wait_recv()
        final_copy(0, c).wait_recv()
        for u in range(CHUNK):
            finish_forward(other + c * CHUNK + u, pr[0, c * CHUNK + u])
        return x

    lax.fori_loop(0, C, forward_other, 0)

    squares = jnp.sum(acc[0].T, axis=0, keepdims=True)
    inners = jnp.sum(acc[1].T, axis=0, keepdims=True)
    which = lax.broadcasted_iota(jnp.int32, (8, T), 0)
    sums = jnp.where(which < 4, squares, inners)
    for j, peer in enumerate(tensor_peers):
        ts[j] = sums
        swap = remote(ts.at[j], tr.at[j], tensor_base + j, peer)
        swap.start()
        swap.wait()
        sums = sums + tr[j]
    width = W * n_tensor
    rscale = lax.rsqrt(sums[0:1] / width + EPSILON)
    inner = rscale * sums[4:5] / width
    rs[...] = jnp.broadcast_to(rscale, (HD, T)).T
    qs[...] = jnp.broadcast_to(rscale * rscale * inner, (HD, T)).T

    def back_chunk(i, x):
        for u in range(CHUNK):
            h = lax.rem(other + i * CHUNK + u, H)
            a = att[:, cols(h)]
            up = g[:, cols(h)].astype(F32)
            gain = gain_ref[pl.ds(h, 1), :]
            unit = a * rs[...]
            lo[:, cols(h)] = (gain * unit).astype(BF16)
            gs[0, pl.ds(h, 1), :] = jnp.sum(up * unit, axis=0, keepdims=True)
            d = (rs[...] * (up * gain) - qs[...] * a).astype(BF16)
            dat[:, cols(h)] = d
            st[1, h] = tn(q[:, cols(h)] * fmb[...], d).astype(BF16)
        state_copy(1, lax.rem((1 - core) * C + i, 2 * C)).start()
        return x

    lax.fori_loop(0, 2 * C, back_chunk, 0)
    out_lo = pltpu.make_async_copy(lo, lo_hbm, out_sem.at[3 * H])
    out_lo.start()

    gain_peers = dp_peers + seq_peers[::-1]

    def gain_copy(j):
        return remote(gs.at[j], gr.at[j], gain_base + j, gain_peers[j])

    gain_copy(0).start()

    def gain_step(j):
        gain_copy(j).wait_recv()
        total = gs[j] + gr[j]
        if j + 1 < len(gain_peers):
            gs[j + 1] = total
            gain_copy(j + 1).start()
        else:
            gg_ref[...] = total

    def out_copy(n, src, dst, h):
        return pltpu.make_async_copy(src.at[:, cols(h)], dst.at[:, cols(h)], out_sem.at[n * H + h])

    def local_backward(h):
        qh, kh, vh, dh = q[:, cols(h)], k[:, cols(h)], v[:, cols(h)], dat[:, cols(h)]
        top = (nt(dh[:T2], vh[:T2]) * mask[:T2, :T2]).astype(BF16)
        low = (nt(dh[T2:], vh) * mask[T2:, :]).astype(BF16)
        into = nt(dh, ci[h]) * fmf[...]
        gq[:T2, cols(h)] = (nn(top, kh[:T2]) + into[:T2]).astype(BF16)
        gq[T2:, cols(h)] = (nn(low, kh) + into[T2:]).astype(BF16)
        out_copy(0, gq, gq_hbm, h).start()
        att[:T2, cols(h)] = tn(top, qh[:T2]) + tn(low[:, :T2], qh[T2:])
        att[T2:, cols(h)] = tn(low[:, T2:], qh[T2:])
        stop, slow = scr[h, :T2, :T2], scr[h, T2:, :]
        gvp[:T2, cols(h)] = tn(stop, dh[:T2]) + tn(slow[:, :T2], dh[T2:])
        gvp[T2:, cols(h)] = tn(slow[:, T2:], dh[T2:])

    interleave(
        1, bwd, local_backward, 4,
        [functools.partial(gain_step, j) for j in range(len(gain_peers))],
    )

    def finish_backward(h, pre):
        carry = (b_state * sr[1, h].astype(F32) + b_pre * pre.astype(F32)).astype(BF16)
        gk[:, cols(h)] = (att[:, cols(h)] + lmf[...] * nt(v[:, cols(h)], carry)).astype(BF16)
        gv[:, cols(h)] = (gvp[:, cols(h)] + lmf[...] * nn(k[:, cols(h)], carry)).astype(BF16)
        out_copy(1, gk, gk_hbm, h).start()
        out_copy(2, gv, gv_hbm, h).start()

    def backward_mine(i, x):
        finish_backward(mine + i, pf[1, i])
        return x

    lax.fori_loop(0, half, backward_mine, 0)

    def backward_other(c, x):
        state_copy(1, (1 - core) * C + c).wait_recv()
        final_copy(1, c).wait_recv()
        for u in range(CHUNK):
            finish_backward(other + c * CHUNK + u, pr[1, c * CHUNK + u])
        return x

    lax.fori_loop(0, C, backward_other, 0)

    for w in range(2):
        def drain(c, x, w=w):
            state_copy(w, c).wait_send()
            state_copy(w, C + c).wait_send()
            for j in range(J):
                step_copy(w, j, c).wait_send()
            final_copy(w, c).wait_send()
            return x

        lax.fori_loop(0, C, drain, 0)
    for j in range(len(gain_peers)):
        gain_copy(j).wait_send()
    out_lo.wait()

    def drain_out(h, x):
        out_copy(0, gq, gq_hbm, h).wait()
        out_copy(1, gk, gk_hbm, h).wait()
        out_copy(2, gv, gv_hbm, h).wait()
        return x

    lax.fori_loop(0, H, drain_out, 0)


def body(sizes, queries, keys, values, grad_out, doc_lengths, gain):
    n_dp, n_seq, n_tensor = sizes
    _, T, W = queries.shape
    H = W // HD
    half = H // 2
    C = half // CHUNK
    J = bits_of(n_seq) - 1
    docs = doc_lengths.shape[1]
    per = (3 + J) * C
    n_gain = bits_of(n_dp) + bits_of(n_seq)
    n_copy = 2 * per + bits_of(n_tensor) + n_gain
    big = jax.ShapeDtypeStruct((T, W), BF16)
    anywhere = pl.BlockSpec(memory_space=pl.ANY)
    vmem = pl.BlockSpec(memory_space=pltpu.VMEM)
    wide = pltpu.VMEM((T, W), BF16)
    wide32 = pltpu.VMEM((T, W), F32)
    column = pltpu.VMEM((T, HD), F32)
    column16 = pltpu.VMEM((T, HD), BF16)
    outs = pl.pallas_call(
        functools.partial(kernel, (n_dp, n_seq, n_tensor, docs)),
        out_shape=(big, big, big, big, jax.ShapeDtypeStruct((H, HD), F32)),
        in_specs=[pl.BlockSpec(memory_space=pltpu.SMEM)] + [anywhere] * 4 + [vmem],
        out_specs=[anywhere] * 4 + [vmem],
        scratch_shapes=[
            wide, wide, wide, wide,
            wide32, wide32,
            pltpu.VMEM((H, T, T), BF16),
            wide, wide, wide, wide, wide,
            pltpu.VMEM((T, T), F32),
            column, column, column16, column16,
            pltpu.VMEM((2, T, HD), F32),
            column, column,
            pltpu.VMEM((2, H, HD, HD), BF16),
            pltpu.VMEM((2, H, HD, HD), BF16),
            pltpu.VMEM((2, J, half, HD, HD), BF16),
            pltpu.VMEM((2, J, half, HD, HD), BF16),
            pltpu.VMEM((half, HD, HD), F32),
            pltpu.VMEM((2, half, HD, HD), BF16),
            pltpu.VMEM((2, half, HD, HD), BF16),
            pltpu.VMEM((H, HD, HD), BF16),
            pltpu.VMEM((bits_of(n_tensor), 8, T), F32),
            pltpu.VMEM((bits_of(n_tensor), 8, T), F32),
            pltpu.VMEM((n_gain, H, HD), F32),
            pltpu.VMEM((n_gain, H, HD), F32),
            pltpu.SemaphoreType.DMA((4,)),
            pltpu.SemaphoreType.DMA((3 * H + 1,)),
            pltpu.SemaphoreType.DMA((n_copy,)),
            pltpu.SemaphoreType.DMA((n_copy,)),
        ],
        compiler_params=pltpu.CompilerParams(
            collective_id=0, has_side_effects=True, vmem_limit_bytes=60 * 1024 * 1024
        ),
        cost_estimate=pl.CostEstimate(
            flops=16 * T * T * W, bytes_accessed=16 * T * W, transcendentals=0
        ),
    )(doc_lengths, queries[0], keys[0], values[0], grad_out[0], gain.reshape(H, HD))
    lo, gq, gk, gv, gg = outs
    return lo[None], gq[None], gk[None], gv[None], gg.reshape(W)


def solution(mesh):
    big = P("dp", "seq", "tensor")
    sizes = tuple(mesh.shape[axis] for axis in ("dp", "seq", "tensor"))
    return jax.shard_map(
        functools.partial(body, sizes),
        mesh=mesh,
        in_specs=(big, big, big, big, P("dp", None), P("tensor")),
        out_specs=(big, big, big, big, P("tensor")),
        check_vma=False,
    )
```

```python
import functools

import jax
import jax.numpy as jnp
from jax import lax
from jax.experimental import pallas as pl
from jax.experimental.pallas import tpu as pltpu
from jax.sharding import PartitionSpec as P

HD = 128
CHUNK = 2
PAIR = 2
EPSILON = 1e-05
MESH = pl.DeviceIdType.MESH
F32 = jnp.float32
BF16 = jnp.bfloat16


def nn(a, b):
    return lax.dot_general(a, b, (((1,), (0,)), ((), ())), preferred_element_type=F32)


def nt(a, b):
    return lax.dot_general(a, b, (((1,), (1,)), ((), ())), preferred_element_type=F32)


def tn(a, b):
    return lax.dot_general(a, b, (((0,), (0,)), ((), ())), preferred_element_type=F32)


def cols(h):
    return pl.ds(pl.multiple_of(h * HD, PAIR * HD), PAIR * HD)


def parts(wide):
    return [wide[:, u * HD:(u + 1) * HD] for u in range(PAIR)]


def joined(pieces):
    return jnp.concatenate(pieces, axis=1)


def bits_of(n):
    return n.bit_length() - 1


def kernel(
    sizes, len_ref, q_hbm, k_hbm, v_hbm, g_hbm, gain_ref,
    lo_hbm, gq_hbm, gk_hbm, gv_hbm, gg_ref, cb, lmf,
    q, k, v, g, att, scr, dat, lo, gq, gk, gv, mask, fmf, fmb, lmb,
    acc, rs, qs, st, sr, sa, rr, pacc, pf, pr, ci, ts, tr, gs, gr,
    in_sem, out_sem, ssem, rsem,
):
    n_dp, n_seq, n_tensor, docs = sizes
    T, W = q.shape
    H = W // HD
    half = H // 2
    C = half // CHUNK
    J = bits_of(n_seq) - 1
    T2 = T // 2
    per = (3 + J) * C
    tensor_base = 2 * per
    gain_base = tensor_base + bits_of(n_tensor)

    loads = [
        pltpu.make_async_copy(src, dst, in_sem.at[i])
        for i, (src, dst) in enumerate(((k_hbm, k), (v_hbm, v), (q_hbm, q), (g_hbm, g)))
    ]
    for load in loads:
        load.start()

    me = lax.axis_index("seq")
    dp = lax.axis_index("dp")
    ten = lax.axis_index("tensor")

    def flip(index, j):
        bit = lax.rem(lax.div(index, 1 << j), 2)
        return index + (1 - 2 * bit) * (1 << j)

    seq_peers = [{"seq": flip(me, j)} for j in range(J + 1)]
    dp_peers = [{"dp": flip(dp, j)} for j in range(bits_of(n_dp))]
    tensor_peers = [{"tensor": flip(ten, j)} for j in range(bits_of(n_tensor))]
    peers = seq_peers + dp_peers + tensor_peers
    barrier = pltpu.get_barrier_semaphore()
    for peer in peers:
        pl.semaphore_signal(barrier, inc=1, device_id=peer, device_id_type=MESH)

    core = lax.rem(me, 2)
    mine = core * half
    other = (1 - core) * half
    begin = me * T

    starts = []
    run = jnp.int32(0)
    for d in range(docs):
        starts.append(run)
        run = run + len_ref[0, d]
    ends = starts[1:] + [run]

    def first_start(pos):
        best = jnp.int32(0)
        for s in starts:
            best = jnp.maximum(best, jnp.where(s <= pos, s, 0))
        return best

    def last_end(pos):
        best = run
        for e in ends:
            best = jnp.minimum(best, jnp.where(e > pos, e, run))
        return best

    def flag(cond):
        return jnp.where(cond, 1.0, 0.0).astype(F32)

    bit_of = [lax.rem(lax.div(me, 1 << j), 2) for j in range(J + 1)]
    fwd, bwd = [], []
    chip = (me - core) * T
    for j in range(J + 1):
        size = 2 << j
        low = lax.div(me, size) * size
        mid = (low + (1 << j)) * T
        high = (low + size) * T
        wf = flag(first_start(high) < mid)
        wb = flag(last_end(low * T - 1) > mid)
        right = flag(bit_of[j] == 1)
        left = 1.0 - right
        fwd.append((
            right + left * wf, left + right * wf,
            right * flag(first_start(chip) < mid),
        ))
        bwd.append((
            left + right * wb, right + left * wb,
            left * flag(last_end(chip + 2 * T - 1) > mid),
        ))
    is_one = flag(core == 1)
    is_zero = 1.0 - is_one
    f_state = is_one * flag(first_start(begin) < begin)
    f_pre = is_zero + is_one * flag(first_start(begin) < chip)
    b_state = is_zero * flag(last_end(begin + T - 1) > begin + T)
    b_pre = is_one + is_zero * flag(last_end(begin + T - 1) > chip + 2 * T)

    row = lax.broadcasted_iota(jnp.int32, (T, HD), 0) + begin
    own_start = first_start(begin)
    keep_first = (row < last_end(begin)) & (own_start < begin)
    keep_last = row >= first_start(begin + T - 1)
    fm = jnp.where(keep_first, 1.0, 0.0).astype(F32)
    lm = jnp.where(keep_last, 1.0, 0.0).astype(F32)
    fmf[...] = fm
    lmf[...] = lm
    fmb[...] = fm.astype(BF16)
    lmb[...] = lm.astype(BF16)
    for r in range(T // HD):
        t_pos = lax.broadcasted_iota(jnp.int32, (HD, T), 0) + (begin + r * HD)
        s_pos = lax.broadcasted_iota(jnp.int32, (HD, T), 1) + begin
        t_start = jnp.zeros((HD, T), jnp.int32)
        for s in starts:
            t_start = jnp.maximum(t_start, jnp.where(t_pos >= s, s, 0))
        inside = (s_pos <= t_pos) & (s_pos >= t_start)
        mask[r * HD:(r + 1) * HD, :] = jnp.where(inside, 1.0, 0.0).astype(F32)

    def remote(src, dst, index, peer):
        return pltpu.make_async_remote_copy(
            src_ref=src, dst_ref=dst, send_sem=ssem.at[index], recv_sem=rsem.at[index],
            device_id=peer, device_id_type=MESH,
        )

    def chunk(c):
        return pl.ds(c * CHUNK, CHUNK)

    def state_copy(w, cc):
        return remote(st.at[w, chunk(cc)], sr.at[w, chunk(cc)], w * per + cc, seq_peers[0])

    def step_copy(w, j, c):
        return remote(
            sa.at[w, j, chunk(c)], rr.at[w, j, chunk(c)],
            w * per + (2 + j) * C + c, seq_peers[j + 1],
        )

    def final_copy(w, c):
        return remote(pf.at[w, chunk(c)], pr.at[w, chunk(c)], w * per + (2 + J) * C + c, seq_peers[0])

    def begin_step(w, coef, c):
        cc = core * C + c
        state_copy(w, cc).wait_recv()
        own, theirs = st[w, chunk(cc)].astype(F32), sr[w, chunk(cc)].astype(F32)
        sa[w, 0, chunk(c)] = (coef[0][0] * own + coef[0][1] * theirs).astype(BF16)
        step_copy(w, 0, c).start()

    def step(w, coef, j, c):
        step_copy(w, j, c).wait_recv()
        got = rr[w, j, chunk(c)].astype(F32)
        keep = coef[j + 1]
        total = keep[2] * got
        if j > 0:
            total = total + pacc[chunk(c)]
        if j < J - 1:
            pacc[chunk(c)] = total
            new = keep[0] * sa[w, j, chunk(c)].astype(F32) + keep[1] * got
            sa[w, j + 1, chunk(c)] = new.astype(BF16)
            step_copy(w, j + 1, c).start()
        else:
            pf[w, chunk(c)] = total.astype(BF16)
            final_copy(w, c).start()

    def interleave(w, coef, work, before, extra):
        order = sorted(
            [(c + j, -j, c) for j in range(J) for c in range(C)]
        )
        events = [functools.partial(begin_step, w, coef, c) for c in range(C)]
        first = len(events)
        events += [functools.partial(step, w, coef, -mj, c) for _, mj, c in order]
        done = 0

        def to(upto):
            nonlocal done
            upto = upto // PAIR * PAIR
            if upto > done:
                lax.fori_loop(done // PAIR, upto // PAIR, lambda i, x: (work(i * PAIR), x)[1], 0)
                done = upto

        to(before)
        later = len(events) - first
        for i, event in enumerate(events):
            if i >= first:
                to(before + ((H - before) * (i - first + 1)) // later)
            event()
            if extra and i >= first and (i - first) % 2 == 1:
                extra.pop(0)()
        to(H)
        while extra:
            extra.pop(0)()

    loads[0].wait()
    loads[1].wait()
    pl.semaphore_wait(barrier, len(peers))

    def state_chunk(i, x):
        h = lax.rem(other + i * CHUNK, H)
        ks, vs = parts(k[:, cols(h)]), parts(v[:, cols(h)])
        new = [tn(kk * lmb[...], vv).astype(BF16) for kk, vv in zip(ks, vs)]
        for u in range(PAIR):
            st[0, h + u] = new[u]
        state_copy(0, lax.rem((1 - core) * C + i, 2 * C)).start()
        return x

    lax.fori_loop(0, 2 * C, state_chunk, 0)
    loads[2].wait()

    def local_forward(h):
        qs_, ks_, vs_ = parts(q[:, cols(h)]), parts(k[:, cols(h)]), parts(v[:, cols(h)])
        top = [(nt(a[:T2], b[:T2]) * mask[:T2, :T2]).astype(BF16) for a, b in zip(qs_, ks_)]
        low = [(nt(a[T2:], b) * mask[T2:, :]).astype(BF16) for a, b in zip(qs_, ks_)]
        up = [nn(a, b[:T2]) for a, b in zip(top, vs_)]
        down = [nn(a, b) for a, b in zip(low, vs_)]
        for u in range(PAIR):
            scr[h + u, :T2, :T2] = top[u]
            scr[h + u, T2:, :] = low[u]
        att[:T2, cols(h)] = joined(up)
        att[T2:, cols(h)] = joined(down)

    interleave(0, fwd, local_forward, 2, [])
    loads[3].wait()
    acc[...] = jnp.zeros_like(acc)

    def finish_forward(h, pre):
        carry = [
            (f_state * sr[0, h + u].astype(F32) + f_pre * pre[u].astype(F32)).astype(BF16)
            for u in range(PAIR)
        ]
        old, up = parts(att[:, cols(h)]), parts(g[:, cols(h)])
        query = parts(q[:, cols(h)])
        gains = [gain_ref[pl.ds(h + u, 1), :] for u in range(PAIR)]
        x = [old[u] + fmf[...] * nn(query[u], carry[u]) for u in range(PAIR)]
        squares = sum(x[u] * x[u] for u in range(PAIR))
        inners = sum((up[u].astype(F32) * gains[u]) * x[u] for u in range(PAIR))
        acc[0] += squares
        acc[1] += inners
        for u in range(PAIR):
            ci[h + u] = carry[u]
        att[:, cols(h)] = joined(x)

    def forward_mine(i, x):
        finish_forward(mine + i * PAIR, [pf[0, i * PAIR + u] for u in range(PAIR)])
        return x

    lax.fori_loop(0, half // PAIR, forward_mine, 0)

    def forward_other(c, x):
        state_copy(0, (1 - core) * C + c).wait_recv()
        final_copy(0, c).wait_recv()
        finish_forward(other + c * PAIR, [pr[0, c * PAIR + u] for u in range(PAIR)])
        return x

    lax.fori_loop(0, C, forward_other, 0)

    squares = jnp.sum(acc[0].T, axis=0, keepdims=True)
    inners = jnp.sum(acc[1].T, axis=0, keepdims=True)
    which = lax.broadcasted_iota(jnp.int32, (8, T), 0)
    sums = jnp.where(which < 4, squares, inners)
    for j, peer in enumerate(tensor_peers):
        ts[j] = sums
        swap = remote(ts.at[j], tr.at[j], tensor_base + j, peer)
        swap.start()
        swap.wait()
        sums = sums + tr[j]
    width = W * n_tensor
    rscale = lax.rsqrt(sums[0:1] / width + EPSILON)
    inner = rscale * sums[4:5] / width
    rs[...] = jnp.broadcast_to(rscale, (HD, T)).T
    qs[...] = jnp.broadcast_to(rscale * rscale * inner, (HD, T)).T

    def back_chunk(i, x):
        h = lax.rem(other + i * CHUNK, H)
        old = parts(att[:, cols(h)])
        ups = [p.astype(F32) for p in parts(g[:, cols(h)])]
        query = parts(q[:, cols(h)])
        gains = [gain_ref[pl.ds(h + u, 1), :] for u in range(PAIR)]
        unit = [old[u] * rs[...] for u in range(PAIR)]
        out = [(gains[u] * unit[u]).astype(BF16) for u in range(PAIR)]
        gsum = [jnp.sum(ups[u] * unit[u], axis=0, keepdims=True) for u in range(PAIR)]
        d = [
            (rs[...] * (ups[u] * gains[u]) - qs[...] * old[u]).astype(BF16)
            for u in range(PAIR)
        ]
        new = [tn(query[u] * fmb[...], d[u]).astype(BF16) for u in range(PAIR)]
        lo[:, cols(h)] = joined(out)
        dat[:, cols(h)] = joined(d)
        for u in range(PAIR):
            gs[0, pl.ds(h + u, 1), :] = gsum[u]
            st[1, h + u] = new[u]
        state_copy(1, lax.rem((1 - core) * C + i, 2 * C)).start()
        return x

    lax.fori_loop(0, 2 * C, back_chunk, 0)
    out_lo = pltpu.make_async_copy(lo, lo_hbm, out_sem.at[3 * H])
    out_lo.start()

    gain_peers = dp_peers + seq_peers[::-1]

    def gain_copy(j):
        return remote(gs.at[j], gr.at[j], gain_base + j, gain_peers[j])

    gain_copy(0).start()

    def gain_step(j):
        gain_copy(j).wait_recv()
        total = gs[j] + gr[j]
        if j + 1 < len(gain_peers):
            gs[j + 1] = total
            gain_copy(j + 1).start()
        else:
            gg_ref[...] = total

    def out_copy(n, src, dst, h):
        return pltpu.make_async_copy(src.at[:, cols(h)], dst.at[:, cols(h)], out_sem.at[n * H + h])

    def local_backward(h):
        qs_, ks_, vs_ = parts(q[:, cols(h)]), parts(k[:, cols(h)]), parts(v[:, cols(h)])
        ds_ = parts(dat[:, cols(h)])
        two = range(PAIR)
        stop = [scr[h + u, :T2, :T2] for u in two]
        slow = [scr[h + u, T2:, :] for u in two]
        carry = [ci[h + u] for u in two]
        top = [(nt(ds_[u][:T2], vs_[u][:T2]) * mask[:T2, :T2]).astype(BF16) for u in two]
        low = [(nt(ds_[u][T2:], vs_[u]) * mask[T2:, :]).astype(BF16) for u in two]
        v_up = [tn(stop[u], ds_[u][:T2]) + tn(slow[u][:, :T2], ds_[u][T2:]) for u in two]
        v_down = [tn(slow[u][:, T2:], ds_[u][T2:]) for u in two]
        into = [nt(ds_[u], carry[u]) * fmf[...] for u in two]
        q_up = [nn(top[u], ks_[u][:T2]) + into[u][:T2] for u in two]
        q_down = [nn(low[u], ks_[u]) + into[u][T2:] for u in two]
        k_up = [tn(top[u], qs_[u][:T2]) + tn(low[u][:, :T2], qs_[u][T2:]) for u in two]
        k_down = [tn(low[u][:, T2:], qs_[u][T2:]) for u in two]
        gv[:T2, cols(h)] = joined(v_up).astype(BF16)
        gv[T2:, cols(h)] = joined(v_down).astype(BF16)
        gq[:T2, cols(h)] = joined(q_up).astype(BF16)
        gq[T2:, cols(h)] = joined(q_down).astype(BF16)
        gk[:T2, cols(h)] = joined(k_up).astype(BF16)
        gk[T2:, cols(h)] = joined(k_down).astype(BF16)
        out_copy(0, gq, gq_hbm, h).start()
        out_copy(1, gk, gk_hbm, h).start()
        out_copy(2, gv, gv_hbm, h).start()

    interleave(
        1, bwd, local_backward, 4,
        [functools.partial(gain_step, j) for j in range(len(gain_peers))],
    )

    def finish_backward(h, pre):
        carry = [
            (b_state * sr[1, h + u].astype(F32) + b_pre * pre[u].astype(F32)).astype(BF16)
            for u in range(PAIR)
        ]
        for u in range(PAIR):
            cb[h + u] = carry[u]

    def backward_mine(i, x):
        finish_backward(mine + i * PAIR, [pf[1, i * PAIR + u] for u in range(PAIR)])
        return x

    lax.fori_loop(0, half // PAIR, backward_mine, 0)

    def backward_other(c, x):
        state_copy(1, (1 - core) * C + c).wait_recv()
        final_copy(1, c).wait_recv()
        finish_backward(other + c * PAIR, [pr[1, c * PAIR + u] for u in range(PAIR)])
        return x

    lax.fori_loop(0, C, backward_other, 0)

    for w in range(2):
        def drain(c, x, w=w):
            state_copy(w, c).wait_send()
            state_copy(w, C + c).wait_send()
            for j in range(J):
                step_copy(w, j, c).wait_send()
            final_copy(w, c).wait_send()
            return x

        lax.fori_loop(0, C, drain, 0)
    for j in range(len(gain_peers)):
        gain_copy(j).wait_send()
    out_lo.wait()

    def drain_out(i, x):
        h = i * PAIR
        out_copy(0, gq, gq_hbm, h).wait()
        out_copy(1, gk, gk_hbm, h).wait()
        out_copy(2, gv, gv_hbm, h).wait()
        return x

    lax.fori_loop(0, H // PAIR, drain_out, 0)


def finish_kernel(lo_in, gq_in, gk_in, gv_in, k, v, cb, lm, gg_in, lo, gq, gk, gv, gg):
    lo[...] = lo_in[...]
    gq[...] = gq_in[...]
    gg[...] = gg_in[...]
    ks, vs = parts(k[...]), parts(v[...])
    more_k = joined([lm[...] * nt(vs[u], cb[u]) for u in range(PAIR)])
    more_v = joined([lm[...] * nn(ks[u], cb[u]) for u in range(PAIR)])
    gk[...] = (gk_in[...].astype(F32) + more_k).astype(BF16)
    gv[...] = (gv_in[...].astype(F32) + more_v).astype(BF16)


def body(sizes, queries, keys, values, grad_out, doc_lengths, gain):
    n_dp, n_seq, n_tensor = sizes
    _, T, W = queries.shape
    H = W // HD
    half = H // 2
    C = half // CHUNK
    J = bits_of(n_seq) - 1
    docs = doc_lengths.shape[1]
    per = (3 + J) * C
    n_gain = bits_of(n_dp) + bits_of(n_seq)
    n_copy = 2 * per + bits_of(n_tensor) + n_gain
    big = jax.ShapeDtypeStruct((T, W), BF16)
    anywhere = pl.BlockSpec(memory_space=pl.ANY)
    vmem = pl.BlockSpec(memory_space=pltpu.VMEM)
    wide = pltpu.VMEM((T, W), BF16)
    wide32 = pltpu.VMEM((T, W), F32)
    args = (queries[0], keys[0], values[0], grad_out[0], gain.reshape(H, HD))
    sums = jax.ShapeDtypeStruct((H, HD), F32)
    carries = jax.ShapeDtypeStruct((H, HD, HD), BF16)
    rows = jax.ShapeDtypeStruct((T, HD), F32)
    column = pltpu.VMEM((T, HD), F32)
    column16 = pltpu.VMEM((T, HD), BF16)
    outs = pl.pallas_call(
        functools.partial(kernel, (n_dp, n_seq, n_tensor, docs)),
        out_shape=(big, big, big, big, sums, carries, rows),
        in_specs=[pl.BlockSpec(memory_space=pltpu.SMEM)] + [anywhere] * 4 + [vmem],
        out_specs=[anywhere] * 4 + [vmem] * 3,
        scratch_shapes=[
            wide, wide, wide, wide,
            wide32,
            pltpu.VMEM((H, T, T), BF16),
            wide, wide, wide, wide, wide,
            pltpu.VMEM((T, T), F32),
            column, column16, column16,
            pltpu.VMEM((2, T, HD), F32),
            column, column,
            pltpu.VMEM((2, H, HD, HD), BF16),
            pltpu.VMEM((2, H, HD, HD), BF16),
            pltpu.VMEM((2, J, half, HD, HD), BF16),
            pltpu.VMEM((2, J, half, HD, HD), BF16),
            pltpu.VMEM((half, HD, HD), F32),
            pltpu.VMEM((2, half, HD, HD), BF16),
            pltpu.VMEM((2, half, HD, HD), BF16),
            pltpu.VMEM((H, HD, HD), BF16),
            pltpu.VMEM((bits_of(n_tensor), 8, T), F32),
            pltpu.VMEM((bits_of(n_tensor), 8, T), F32),
            pltpu.VMEM((n_gain, H, HD), F32),
            pltpu.VMEM((n_gain, H, HD), F32),
            pltpu.SemaphoreType.DMA((4,)),
            pltpu.SemaphoreType.DMA((3 * H + 1,)),
            pltpu.SemaphoreType.DMA((n_copy,)),
            pltpu.SemaphoreType.DMA((n_copy,)),
        ],
        compiler_params=pltpu.CompilerParams(
            collective_id=0, has_side_effects=True, vmem_limit_bytes=60 * 1024 * 1024
        ),
        cost_estimate=pl.CostEstimate(
            flops=16 * T * T * W, bytes_accessed=16 * T * W, transcendentals=0
        ),
    )(doc_lengths, *args)
    lo, gq, gk, gv, gg, cb, lm = outs
    block = pl.BlockSpec((T, PAIR * HD), lambda i: (0, i))
    whole = pl.BlockSpec((H, HD), lambda i: (0, 0))
    lo, gq, gk, gv, gg = pl.pallas_call(
        finish_kernel,
        grid=(H // PAIR,),
        out_shape=(big, big, big, big, sums),
        in_specs=[block] * 6 + [
            pl.BlockSpec((PAIR, HD, HD), lambda i: (i, 0, 0)),
            pl.BlockSpec((T, HD), lambda i: (0, 0)),
            whole,
        ],
        out_specs=[block] * 4 + [whole],
        compiler_params=pltpu.CompilerParams(vmem_limit_bytes=60 * 1024 * 1024),
        cost_estimate=pl.CostEstimate(
            flops=4 * T * W * HD, bytes_accessed=20 * T * W, transcendentals=0
        ),
    )(lo, gq, gk, gv, keys[0], values[0], cb, lm, gg)
    return lo[None], gq[None], gk[None], gv[None], gg.reshape(W)


def solution(mesh):
    big = P("dp", "seq", "tensor")
    sizes = tuple(mesh.shape[axis] for axis in ("dp", "seq", "tensor"))
    return jax.shard_map(
        functools.partial(body, sizes),
        mesh=mesh,
        in_specs=(big, big, big, big, P("dp", None), P("tensor")),
        out_specs=(big, big, big, big, P("tensor")),
        check_vma=False,
    )
```

```python
import functools

import jax
import jax.numpy as jnp
from jax import lax
from jax.experimental import pallas as pl
from jax.experimental.pallas import tpu as pltpu
from jax.sharding import PartitionSpec as P

HD = 128
CHUNK = 2
PAIR = 2
EPSILON = 1e-05
MESH = pl.DeviceIdType.MESH
F32 = jnp.float32
BF16 = jnp.bfloat16


def nn(a, b):
    return lax.dot_general(a, b, (((1,), (0,)), ((), ())), preferred_element_type=F32)


def nt(a, b):
    return lax.dot_general(a, b, (((1,), (1,)), ((), ())), preferred_element_type=F32)


def tn(a, b):
    return lax.dot_general(a, b, (((0,), (0,)), ((), ())), preferred_element_type=F32)


def cols(h):
    return pl.ds(pl.multiple_of(h * HD, PAIR * HD), PAIR * HD)


def parts(wide):
    return [wide[:, u * HD:(u + 1) * HD] for u in range(PAIR)]


def joined(pieces):
    return jnp.concatenate(pieces, axis=1)


def bits_of(n):
    return n.bit_length() - 1


def kernel(
    sizes, len_ref, q_hbm, k_hbm, v_hbm, g_hbm, gain_ref,
    lo_hbm, gq_hbm, gk_hbm, gv_hbm, gg_ref, cb, lmf,
    q, k, v, g, att, scr, dat, lo, gq, gk, gv, mask, maskt, fmf, fmb, lmb,
    acc, rs, qs, st, sr, sa, rr, pacc, pf, pr, ci, ts, tr, gs, gr,
    in_sem, out_sem, ssem, rsem,
):
    n_dp, n_seq, n_tensor, docs = sizes
    T, W = q.shape
    H = W // HD
    half = H // 2
    C = half // CHUNK
    J = bits_of(n_seq) - 1
    T2 = T // 2
    per = (3 + J) * C
    tensor_base = 2 * per
    gain_base = tensor_base + bits_of(n_tensor)

    loads = [
        pltpu.make_async_copy(src, dst, in_sem.at[i])
        for i, (src, dst) in enumerate(((k_hbm, k), (v_hbm, v), (q_hbm, q), (g_hbm, g)))
    ]
    loads[0].start()
    loads[1].start()

    me = lax.axis_index("seq")
    dp = lax.axis_index("dp")
    ten = lax.axis_index("tensor")

    def flip(index, j):
        bit = lax.rem(lax.div(index, 1 << j), 2)
        return index + (1 - 2 * bit) * (1 << j)

    seq_peers = [{"seq": flip(me, j)} for j in range(J + 1)]
    dp_peers = [{"dp": flip(dp, j)} for j in range(bits_of(n_dp))]
    tensor_peers = [{"tensor": flip(ten, j)} for j in range(bits_of(n_tensor))]
    peers = seq_peers + dp_peers + tensor_peers
    barrier = pltpu.get_barrier_semaphore()
    for peer in peers:
        pl.semaphore_signal(barrier, inc=1, device_id=peer, device_id_type=MESH)

    core = lax.rem(me, 2)
    mine = core * half
    other = (1 - core) * half
    begin = me * T

    starts = []
    run = jnp.int32(0)
    for d in range(docs):
        starts.append(run)
        run = run + len_ref[0, d]
    ends = starts[1:] + [run]

    def first_start(pos):
        best = jnp.int32(0)
        for s in starts:
            best = jnp.maximum(best, jnp.where(s <= pos, s, 0))
        return best

    def last_end(pos):
        best = run
        for e in ends:
            best = jnp.minimum(best, jnp.where(e > pos, e, run))
        return best

    def flag(cond):
        return jnp.where(cond, 1.0, 0.0).astype(F32)

    bit_of = [lax.rem(lax.div(me, 1 << j), 2) for j in range(J + 1)]
    fwd, bwd = [], []
    chip = (me - core) * T
    for j in range(J + 1):
        size = 2 << j
        low = lax.div(me, size) * size
        mid = (low + (1 << j)) * T
        high = (low + size) * T
        wf = flag(first_start(high) < mid)
        wb = flag(last_end(low * T - 1) > mid)
        right = flag(bit_of[j] == 1)
        left = 1.0 - right
        fwd.append((
            right + left * wf, left + right * wf,
            right * flag(first_start(chip) < mid),
        ))
        bwd.append((
            left + right * wb, right + left * wb,
            left * flag(last_end(chip + 2 * T - 1) > mid),
        ))
    is_one = flag(core == 1)
    is_zero = 1.0 - is_one
    f_state = is_one * flag(first_start(begin) < begin)
    f_pre = is_zero + is_one * flag(first_start(begin) < chip)
    b_state = is_zero * flag(last_end(begin + T - 1) > begin + T)
    b_pre = is_one + is_zero * flag(last_end(begin + T - 1) > chip + 2 * T)

    row = lax.broadcasted_iota(jnp.int32, (T, HD), 0) + begin
    own_start = first_start(begin)
    keep_first = (row < last_end(begin)) & (own_start < begin)
    keep_last = row >= first_start(begin + T - 1)
    fm = jnp.where(keep_first, 1.0, 0.0).astype(F32)
    lm = jnp.where(keep_last, 1.0, 0.0).astype(F32)
    fmf[...] = fm
    lmf[...] = lm
    fmb[...] = fm.astype(BF16)
    lmb[...] = lm.astype(BF16)
    for r in range(T // HD):
        t_pos = lax.broadcasted_iota(jnp.int32, (HD, T), 0) + (begin + r * HD)
        s_pos = lax.broadcasted_iota(jnp.int32, (HD, T), 1) + begin
        t_start = jnp.zeros((HD, T), jnp.int32)
        for s in starts:
            t_start = jnp.maximum(t_start, jnp.where(t_pos >= s, s, 0))
        inside = (s_pos <= t_pos) & (s_pos >= t_start)
        mask[r * HD:(r + 1) * HD, :] = jnp.where(inside, 1.0, 0.0).astype(F32)
        c_start = jnp.zeros((HD, T), jnp.int32)
        for s in starts:
            c_start = jnp.maximum(c_start, jnp.where(s_pos >= s, s, 0))
        inside = (t_pos <= s_pos) & (t_pos >= c_start)
        maskt[r * HD:(r + 1) * HD, :] = jnp.where(inside, 1.0, 0.0).astype(F32)

    def remote(src, dst, index, peer):
        return pltpu.make_async_remote_copy(
            src_ref=src, dst_ref=dst, send_sem=ssem.at[index], recv_sem=rsem.at[index],
            device_id=peer, device_id_type=MESH,
        )

    def chunk(c):
        return pl.ds(c * CHUNK, CHUNK)

    def state_copy(w, cc):
        return remote(st.at[w, chunk(cc)], sr.at[w, chunk(cc)], w * per + cc, seq_peers[0])

    def step_copy(w, j, c):
        return remote(
            sa.at[w, j, chunk(c)], rr.at[w, j, chunk(c)],
            w * per + (2 + j) * C + c, seq_peers[j + 1],
        )

    def final_copy(w, c):
        return remote(pf.at[w, chunk(c)], pr.at[w, chunk(c)], w * per + (2 + J) * C + c, seq_peers[0])

    def begin_step(w, coef, c):
        cc = core * C + c
        state_copy(w, cc).wait_recv()
        own, theirs = st[w, chunk(cc)].astype(F32), sr[w, chunk(cc)].astype(F32)
        sa[w, 0, chunk(c)] = (coef[0][0] * own + coef[0][1] * theirs).astype(BF16)
        step_copy(w, 0, c).start()

    def step(w, coef, j, c):
        step_copy(w, j, c).wait_recv()
        got = rr[w, j, chunk(c)].astype(F32)
        keep = coef[j + 1]
        total = keep[2] * got
        if j > 0:
            total = total + pacc[chunk(c)]
        if j < J - 1:
            pacc[chunk(c)] = total
            new = keep[0] * sa[w, j, chunk(c)].astype(F32) + keep[1] * got
            sa[w, j + 1, chunk(c)] = new.astype(BF16)
            step_copy(w, j + 1, c).start()
        else:
            pf[w, chunk(c)] = total.astype(BF16)
            final_copy(w, c).start()

    def interleave(w, coef, work, before, extra):
        order = sorted(
            [(c + j, -j, c) for j in range(J) for c in range(C)]
        )
        events = [functools.partial(begin_step, w, coef, c) for c in range(C)]
        first = len(events)
        events += [functools.partial(step, w, coef, -mj, c) for _, mj, c in order]
        done = 0

        def to(upto):
            nonlocal done
            upto = upto // PAIR * PAIR
            if upto > done:
                lax.fori_loop(done // PAIR, upto // PAIR, lambda i, x: (work(i * PAIR), x)[1], 0)
                done = upto

        to(before)
        later = len(events) - first
        for i, event in enumerate(events):
            if i >= first:
                to(before + ((H - before) * (i - first + 1)) // later)
            event()
            if extra and i >= first and (i - first) % 2 == 1:
                extra.pop(0)()
        to(H)
        while extra:
            extra.pop(0)()

    loads[0].wait()
    loads[1].wait()
    loads[2].start()
    loads[3].start()
    pl.semaphore_wait(barrier, len(peers))

    def state_chunk(i, x):
        h = lax.rem(other + i * CHUNK, H)
        ks, vs = parts(k[:, cols(h)]), parts(v[:, cols(h)])
        new = [tn(kk * lmb[...], vv).astype(BF16) for kk, vv in zip(ks, vs)]
        for u in range(PAIR):
            st[0, h + u] = new[u]
        state_copy(0, lax.rem((1 - core) * C + i, 2 * C)).start()
        return x

    lax.fori_loop(0, 2 * C, state_chunk, 0)
    loads[2].wait()

    def local_forward(h):
        qs_, ks_, vs_ = parts(q[:, cols(h)]), parts(k[:, cols(h)]), parts(v[:, cols(h)])
        top = [(nt(a[:T2], b[:T2]) * mask[:T2, :T2]).astype(BF16) for a, b in zip(qs_, ks_)]
        low = [(nt(a[T2:], b) * mask[T2:, :]).astype(BF16) for a, b in zip(qs_, ks_)]
        up = [nn(a, b[:T2]) for a, b in zip(top, vs_)]
        down = [nn(a, b) for a, b in zip(low, vs_)]
        left = [(nt(a[:T2], b) * maskt[:T2, :]).astype(BF16) for a, b in zip(ks_, qs_)]
        right = [(nt(a[T2:], b[T2:]) * maskt[T2:, T2:]).astype(BF16) for a, b in zip(ks_, qs_)]
        for u in range(PAIR):
            scr[h + u, :T2, :] = left[u]
            scr[h + u, T2:, T2:] = right[u]
        att[:T2, cols(h)] = joined(up)
        att[T2:, cols(h)] = joined(down)

    interleave(0, fwd, local_forward, 2, [])
    loads[3].wait()
    acc[...] = jnp.zeros_like(acc)

    def finish_forward(h, pre):
        carry = [
            (f_state * sr[0, h + u].astype(F32) + f_pre * pre[u].astype(F32)).astype(BF16)
            for u in range(PAIR)
        ]
        old, up = parts(att[:, cols(h)]), parts(g[:, cols(h)])
        query = parts(q[:, cols(h)])
        gains = [gain_ref[pl.ds(h + u, 1), :] for u in range(PAIR)]
        x = [old[u] + fmf[...] * nn(query[u], carry[u]) for u in range(PAIR)]
        squares = sum(x[u] * x[u] for u in range(PAIR))
        inners = sum((up[u].astype(F32) * gains[u]) * x[u] for u in range(PAIR))
        acc[0] += squares
        acc[1] += inners
        for u in range(PAIR):
            ci[h + u] = carry[u]
        att[:, cols(h)] = joined(x)

    def forward_mine(i, x):
        finish_forward(mine + i * PAIR, [pf[0, i * PAIR + u] for u in range(PAIR)])
        return x

    lax.fori_loop(0, half // PAIR, forward_mine, 0)

    def forward_other(c, x):
        state_copy(0, (1 - core) * C + c).wait_recv()
        final_copy(0, c).wait_recv()
        finish_forward(other + c * PAIR, [pr[0, c * PAIR + u] for u in range(PAIR)])
        return x

    lax.fori_loop(0, C, forward_other, 0)

    squares = jnp.sum(acc[0].T, axis=0, keepdims=True)
    inners = jnp.sum(acc[1].T, axis=0, keepdims=True)
    which = lax.broadcasted_iota(jnp.int32, (8, T), 0)
    sums = jnp.where(which < 4, squares, inners)
    for j, peer in enumerate(tensor_peers):
        ts[j] = sums
        swap = remote(ts.at[j], tr.at[j], tensor_base + j, peer)
        swap.start()
        swap.wait()
        sums = sums + tr[j]
    width = W * n_tensor
    rscale = lax.rsqrt(sums[0:1] / width + EPSILON)
    inner = rscale * sums[4:5] / width
    rs[...] = jnp.broadcast_to(rscale, (HD, T)).T
    qs[...] = jnp.broadcast_to(rscale * rscale * inner, (HD, T)).T

    def back_chunk(i, x):
        h = lax.rem(other + i * CHUNK, H)
        old = parts(att[:, cols(h)])
        ups = [p.astype(F32) for p in parts(g[:, cols(h)])]
        query = parts(q[:, cols(h)])
        gains = [gain_ref[pl.ds(h + u, 1), :] for u in range(PAIR)]
        unit = [old[u] * rs[...] for u in range(PAIR)]
        out = [(gains[u] * unit[u]).astype(BF16) for u in range(PAIR)]
        gsum = [jnp.sum(ups[u] * unit[u], axis=0, keepdims=True) for u in range(PAIR)]
        d = [
            (rs[...] * (ups[u] * gains[u]) - qs[...] * old[u]).astype(BF16)
            for u in range(PAIR)
        ]
        new = [tn(query[u] * fmb[...], d[u]).astype(BF16) for u in range(PAIR)]
        lo[:, cols(h)] = joined(out)
        dat[:, cols(h)] = joined(d)
        for u in range(PAIR):
            gs[0, pl.ds(h + u, 1), :] = gsum[u]
            st[1, h + u] = new[u]
        state_copy(1, lax.rem((1 - core) * C + i, 2 * C)).start()
        return x

    lax.fori_loop(0, 2 * C, back_chunk, 0)
    out_lo = pltpu.make_async_copy(lo, lo_hbm, out_sem.at[3 * H])
    out_lo.start()

    gain_peers = dp_peers + seq_peers[::-1]

    def gain_copy(j):
        return remote(gs.at[j], gr.at[j], gain_base + j, gain_peers[j])

    gain_copy(0).start()

    def gain_step(j):
        gain_copy(j).wait_recv()
        total = gs[j] + gr[j]
        if j + 1 < len(gain_peers):
            gs[j + 1] = total
            gain_copy(j + 1).start()
        else:
            gg_ref[...] = total

    def out_copy(n, src, dst, h):
        return pltpu.make_async_copy(src.at[:, cols(h)], dst.at[:, cols(h)], out_sem.at[n * H + h])

    def local_backward(h):
        qs_, ks_, vs_ = parts(q[:, cols(h)]), parts(k[:, cols(h)]), parts(v[:, cols(h)])
        ds_ = parts(dat[:, cols(h)])
        two = range(PAIR)
        s_left = [scr[h + u, :T2, :] for u in two]
        s_right = [scr[h + u, T2:, T2:] for u in two]
        carry = [ci[h + u] for u in two]
        top = [(nt(ds_[u][:T2], vs_[u][:T2]) * mask[:T2, :T2]).astype(BF16) for u in two]
        low = [(nt(ds_[u][T2:], vs_[u]) * mask[T2:, :]).astype(BF16) for u in two]
        left = [(nt(vs_[u][:T2], ds_[u]) * maskt[:T2, :]).astype(BF16) for u in two]
        right = [(nt(vs_[u][T2:], ds_[u][T2:]) * maskt[T2:, T2:]).astype(BF16) for u in two]
        v_up = [nn(s_left[u], ds_[u]) for u in two]
        v_down = [nn(s_right[u], ds_[u][T2:]) for u in two]
        into = [nt(ds_[u], carry[u]) * fmf[...] for u in two]
        q_up = [nn(top[u], ks_[u][:T2]) + into[u][:T2] for u in two]
        q_down = [nn(low[u], ks_[u]) + into[u][T2:] for u in two]
        k_up = [nn(left[u], qs_[u]) for u in two]
        k_down = [nn(right[u], qs_[u][T2:]) for u in two]
        gv[:T2, cols(h)] = joined(v_up).astype(BF16)
        gv[T2:, cols(h)] = joined(v_down).astype(BF16)
        gq[:T2, cols(h)] = joined(q_up).astype(BF16)
        gq[T2:, cols(h)] = joined(q_down).astype(BF16)
        gk[:T2, cols(h)] = joined(k_up).astype(BF16)
        gk[T2:, cols(h)] = joined(k_down).astype(BF16)
        out_copy(0, gq, gq_hbm, h).start()
        out_copy(1, gk, gk_hbm, h).start()
        out_copy(2, gv, gv_hbm, h).start()

    interleave(
        1, bwd, local_backward, 2,
        [functools.partial(gain_step, j) for j in range(len(gain_peers))],
    )

    def finish_backward(h, pre):
        carry = [
            (b_state * sr[1, h + u].astype(F32) + b_pre * pre[u].astype(F32)).astype(BF16)
            for u in range(PAIR)
        ]
        for u in range(PAIR):
            cb[h + u] = carry[u]

    def backward_mine(i, x):
        finish_backward(mine + i * PAIR, [pf[1, i * PAIR + u] for u in range(PAIR)])
        return x

    lax.fori_loop(0, half // PAIR, backward_mine, 0)

    def backward_other(c, x):
        state_copy(1, (1 - core) * C + c).wait_recv()
        final_copy(1, c).wait_recv()
        finish_backward(other + c * PAIR, [pr[1, c * PAIR + u] for u in range(PAIR)])
        return x

    lax.fori_loop(0, C, backward_other, 0)

    for w in range(2):
        def drain(c, x, w=w):
            state_copy(w, c).wait_send()
            state_copy(w, C + c).wait_send()
            for j in range(J):
                step_copy(w, j, c).wait_send()
            final_copy(w, c).wait_send()
            return x

        lax.fori_loop(0, C, drain, 0)
    for j in range(len(gain_peers)):
        gain_copy(j).wait_send()
    out_lo.wait()

    def drain_out(i, x):
        h = i * PAIR
        out_copy(0, gq, gq_hbm, h).wait()
        out_copy(1, gk, gk_hbm, h).wait()
        out_copy(2, gv, gv_hbm, h).wait()
        return x

    lax.fori_loop(0, H // PAIR, drain_out, 0)


def finish_kernel(lo_in, gq_in, gk_in, gv_in, k, v, cb, lm, gg_in, lo, gq, gk, gv, gg):
    lo[...] = lo_in[...]
    gq[...] = gq_in[...]
    gg[...] = gg_in[...]
    for h in range(k.shape[1] // HD):
        here = slice(h * HD, (h + 1) * HD)
        more_k = lm[...] * nt(v[:, here], cb[h])
        more_v = lm[...] * nn(k[:, here], cb[h])
        gk[:, here] = (gk_in[:, here].astype(F32) + more_k).astype(BF16)
        gv[:, here] = (gv_in[:, here].astype(F32) + more_v).astype(BF16)


def body(sizes, queries, keys, values, grad_out, doc_lengths, gain):
    n_dp, n_seq, n_tensor = sizes
    _, T, W = queries.shape
    H = W // HD
    half = H // 2
    C = half // CHUNK
    J = bits_of(n_seq) - 1
    docs = doc_lengths.shape[1]
    per = (3 + J) * C
    n_gain = bits_of(n_dp) + bits_of(n_seq)
    n_copy = 2 * per + bits_of(n_tensor) + n_gain
    big = jax.ShapeDtypeStruct((T, W), BF16)
    anywhere = pl.BlockSpec(memory_space=pl.ANY)
    vmem = pl.BlockSpec(memory_space=pltpu.VMEM)
    wide = pltpu.VMEM((T, W), BF16)
    wide32 = pltpu.VMEM((T, W), F32)
    args = (queries[0], keys[0], values[0], grad_out[0], gain.reshape(H, HD))
    sums = jax.ShapeDtypeStruct((H, HD), F32)
    carries = jax.ShapeDtypeStruct((H, HD, HD), BF16)
    rows = jax.ShapeDtypeStruct((T, HD), F32)
    column = pltpu.VMEM((T, HD), F32)
    column16 = pltpu.VMEM((T, HD), BF16)
    outs = pl.pallas_call(
        functools.partial(kernel, (n_dp, n_seq, n_tensor, docs)),
        out_shape=(big, big, big, big, sums, carries, rows),
        in_specs=[pl.BlockSpec(memory_space=pltpu.SMEM)] + [anywhere] * 4 + [vmem],
        out_specs=[anywhere] * 4 + [vmem] * 3,
        scratch_shapes=[
            wide, wide, wide, wide,
            wide32,
            pltpu.VMEM((H, T, T), BF16),
            wide, wide, wide, wide, wide,
            pltpu.VMEM((T, T), F32),
            pltpu.VMEM((T, T), F32),
            column, column16, column16,
            pltpu.VMEM((2, T, HD), F32),
            column, column,
            pltpu.VMEM((2, H, HD, HD), BF16),
            pltpu.VMEM((2, H, HD, HD), BF16),
            pltpu.VMEM((2, J, half, HD, HD), BF16),
            pltpu.VMEM((2, J, half, HD, HD), BF16),
            pltpu.VMEM((half, HD, HD), F32),
            pltpu.VMEM((2, half, HD, HD), BF16),
            pltpu.VMEM((2, half, HD, HD), BF16),
            pltpu.VMEM((H, HD, HD), BF16),
            pltpu.VMEM((bits_of(n_tensor), 8, T), F32),
            pltpu.VMEM((bits_of(n_tensor), 8, T), F32),
            pltpu.VMEM((n_gain, H, HD), F32),
            pltpu.VMEM((n_gain, H, HD), F32),
            pltpu.SemaphoreType.DMA((4,)),
            pltpu.SemaphoreType.DMA((3 * H + 1,)),
            pltpu.SemaphoreType.DMA((n_copy,)),
            pltpu.SemaphoreType.DMA((n_copy,)),
        ],
        compiler_params=pltpu.CompilerParams(
            collective_id=0, has_side_effects=True, vmem_limit_bytes=60 * 1024 * 1024
        ),
        cost_estimate=pl.CostEstimate(
            flops=16 * T * T * W, bytes_accessed=16 * T * W, transcendentals=0
        ),
    )(doc_lengths, *args)
    lo, gq, gk, gv, gg, cb, lm = outs
    step_rows = min(T, 128)
    block = pl.BlockSpec((step_rows, W), lambda i: (i, 0))
    whole = pl.BlockSpec((H, HD), lambda i: (0, 0))
    lo, gq, gk, gv, gg = pl.pallas_call(
        finish_kernel,
        grid=(T // step_rows,),
        out_shape=(big, big, big, big, sums),
        in_specs=[block] * 6 + [
            pl.BlockSpec((H, HD, HD), lambda i: (0, 0, 0)),
            pl.BlockSpec((step_rows, HD), lambda i: (i, 0)),
            whole,
        ],
        out_specs=[block] * 4 + [whole],
        compiler_params=pltpu.CompilerParams(vmem_limit_bytes=60 * 1024 * 1024),
        cost_estimate=pl.CostEstimate(
            flops=4 * T * W * HD, bytes_accessed=20 * T * W, transcendentals=0
        ),
    )(lo, gq, gk, gv, keys[0], values[0], cb, lm, gg)
    return lo[None], gq[None], gk[None], gv[None], gg.reshape(W)


def solution(mesh):
    big = P("dp", "seq", "tensor")
    sizes = tuple(mesh.shape[axis] for axis in ("dp", "seq", "tensor"))
    return jax.shard_map(
        functools.partial(body, sizes),
        mesh=mesh,
        in_specs=(big, big, big, big, P("dp", None), P("tensor")),
        out_specs=(big, big, big, big, P("tensor")),
        check_vma=False,
    )
```

```python
import functools

import jax
import jax.numpy as jnp
from jax import lax
from jax.experimental import pallas as pl
from jax.experimental.pallas import tpu as pltpu
from jax.sharding import PartitionSpec as P

HD = 128
CHUNK = 2
PAIR = 2
EPSILON = 1e-05
MESH = pl.DeviceIdType.MESH
F32 = jnp.float32
BF16 = jnp.bfloat16


def nn(a, b):
    return lax.dot_general(a, b, (((1,), (0,)), ((), ())), preferred_element_type=F32)


def nt(a, b):
    return lax.dot_general(a, b, (((1,), (1,)), ((), ())), preferred_element_type=F32)


def tn(a, b):
    return lax.dot_general(a, b, (((0,), (0,)), ((), ())), preferred_element_type=F32)


def cols(h):
    return pl.ds(pl.multiple_of(h * HD, PAIR * HD), PAIR * HD)


def parts(wide):
    return [wide[:, u * HD:(u + 1) * HD] for u in range(PAIR)]


def joined(pieces):
    return jnp.concatenate(pieces, axis=1)


def bits_of(n):
    return n.bit_length() - 1


def kernel(
    sizes, len_ref, q_hbm, k_hbm, v_hbm, g_hbm, gain_ref,
    lo_hbm, gq_hbm, gk_hbm, gv_hbm, gg_ref, cb, lmf,
    q, k, v, g, att, scr, dat, lo, gq, gk, gv, mask, fmf, fmb, lmb,
    acc, rs, qs, st, sr, sa, rr, pacc, pf, pr, ci, ts, tr, gs, gr,
    in_sem, out_sem, ssem, rsem,
):
    n_dp, n_seq, n_tensor, docs = sizes
    T, W = q.shape
    H = W // HD
    half = H // 2
    C = half // CHUNK
    J = bits_of(n_seq) - 1
    T2 = T // 2
    per = (3 + J) * C
    tensor_base = 2 * per
    gain_base = tensor_base + bits_of(n_tensor)

    loads = [
        pltpu.make_async_copy(src, dst, in_sem.at[i])
        for i, (src, dst) in enumerate(((k_hbm, k), (v_hbm, v), (q_hbm, q), (g_hbm, g)))
    ]
    loads[0].start()
    loads[1].start()

    me = lax.axis_index("seq")
    dp = lax.axis_index("dp")
    ten = lax.axis_index("tensor")

    def flip(index, j):
        bit = lax.rem(lax.div(index, 1 << j), 2)
        return index + (1 - 2 * bit) * (1 << j)

    seq_peers = [{"seq": flip(me, j)} for j in range(J + 1)]
    dp_peers = [{"dp": flip(dp, j)} for j in range(bits_of(n_dp))]
    tensor_peers = [{"tensor": flip(ten, j)} for j in range(bits_of(n_tensor))]
    peers = seq_peers + dp_peers + tensor_peers
    barrier = pltpu.get_barrier_semaphore()
    for peer in peers:
        pl.semaphore_signal(barrier, inc=1, device_id=peer, device_id_type=MESH)

    core = lax.rem(me, 2)
    mine = core * half
    other = (1 - core) * half
    begin = me * T

    starts = []
    run = jnp.int32(0)
    for d in range(docs):
        starts.append(run)
        run = run + len_ref[0, d]
    ends = starts[1:] + [run]

    def first_start(pos):
        best = jnp.int32(0)
        for s in starts:
            best = jnp.maximum(best, jnp.where(s <= pos, s, 0))
        return best

    def last_end(pos):
        best = run
        for e in ends:
            best = jnp.minimum(best, jnp.where(e > pos, e, run))
        return best

    def flag(cond):
        return jnp.where(cond, 1.0, 0.0).astype(F32)

    bit_of = [lax.rem(lax.div(me, 1 << j), 2) for j in range(J + 1)]
    fwd, bwd = [], []
    chip = (me - core) * T
    for j in range(J + 1):
        size = 2 << j
        low = lax.div(me, size) * size
        mid = (low + (1 << j)) * T
        high = (low + size) * T
        wf = flag(first_start(high) < mid)
        wb = flag(last_end(low * T - 1) > mid)
        right = flag(bit_of[j] == 1)
        left = 1.0 - right
        fwd.append((
            right + left * wf, left + right * wf,
            right * flag(first_start(chip) < mid),
        ))
        bwd.append((
            left + right * wb, right + left * wb,
            left * flag(last_end(chip + 2 * T - 1) > mid),
        ))
    is_one = flag(core == 1)
    is_zero = 1.0 - is_one
    f_state = is_one * flag(first_start(begin) < begin)
    f_pre = is_zero + is_one * flag(first_start(begin) < chip)
    b_state = is_zero * flag(last_end(begin + T - 1) > begin + T)
    b_pre = is_one + is_zero * flag(last_end(begin + T - 1) > chip + 2 * T)

    row = lax.broadcasted_iota(jnp.int32, (T, HD), 0) + begin
    own_start = first_start(begin)
    keep_first = (row < last_end(begin)) & (own_start < begin)
    keep_last = row >= first_start(begin + T - 1)
    fm = jnp.where(keep_first, 1.0, 0.0).astype(F32)
    lm = jnp.where(keep_last, 1.0, 0.0).astype(F32)
    fmf[...] = fm
    lmf[...] = lm
    fmb[...] = fm.astype(BF16)
    lmb[...] = lm.astype(BF16)
    for r in range(T // HD):
        t_pos = lax.broadcasted_iota(jnp.int32, (HD, T), 0) + (begin + r * HD)
        s_pos = lax.broadcasted_iota(jnp.int32, (HD, T), 1) + begin
        t_start = jnp.zeros((HD, T), jnp.int32)
        for s in starts:
            t_start = jnp.maximum(t_start, jnp.where(t_pos >= s, s, 0))
        inside = (s_pos <= t_pos) & (s_pos >= t_start)
        mask[r * HD:(r + 1) * HD, :] = jnp.where(inside, 1.0, 0.0).astype(F32)

    def remote(src, dst, index, peer):
        return pltpu.make_async_remote_copy(
            src_ref=src, dst_ref=dst, send_sem=ssem.at[index], recv_sem=rsem.at[index],
            device_id=peer, device_id_type=MESH,
        )

    def chunk(c):
        return pl.ds(c * CHUNK, CHUNK)

    def state_copy(w, cc):
        return remote(st.at[w, chunk(cc)], sr.at[w, chunk(cc)], w * per + cc, seq_peers[0])

    def step_copy(w, j, c):
        return remote(
            sa.at[w, j, chunk(c)], rr.at[w, j, chunk(c)],
            w * per + (2 + j) * C + c, seq_peers[j + 1],
        )

    def final_copy(w, c):
        return remote(pf.at[w, chunk(c)], pr.at[w, chunk(c)], w * per + (2 + J) * C + c, seq_peers[0])

    def begin_step(w, coef, c):
        cc = core * C + c
        state_copy(w, cc).wait_recv()
        own, theirs = st[w, chunk(cc)].astype(F32), sr[w, chunk(cc)].astype(F32)
        sa[w, 0, chunk(c)] = (coef[0][0] * own + coef[0][1] * theirs).astype(BF16)
        step_copy(w, 0, c).start()

    def step(w, coef, j, c):
        step_copy(w, j, c).wait_recv()
        got = rr[w, j, chunk(c)].astype(F32)
        keep = coef[j + 1]
        total = keep[2] * got
        if j > 0:
            total = total + pacc[chunk(c)]
        if j < J - 1:
            pacc[chunk(c)] = total
            new = keep[0] * sa[w, j, chunk(c)].astype(F32) + keep[1] * got
            sa[w, j + 1, chunk(c)] = new.astype(BF16)
            step_copy(w, j + 1, c).start()
        else:
            pf[w, chunk(c)] = total.astype(BF16)
            final_copy(w, c).start()

    def interleave(w, coef, work, before, extra, after=None):
        order = sorted(
            [(c + j, -j, c) for j in range(J) for c in range(C)]
        )
        events = [(functools.partial(step, w, coef, -mj, c), -mj, c) for _, mj, c in order]
        done = 0

        def to(upto):
            nonlocal done
            upto = upto // PAIR * PAIR
            if upto > done:
                lax.fori_loop(done // PAIR, upto // PAIR, lambda i, x: (work(i * PAIR), x)[1], 0)
                done = upto

        for i, (event, j, c) in enumerate(events):
            to(before + ((H - before) * (i + 1)) // len(events))
            event()
            if j == J - 1 and after is not None:
                after(c)
            if extra and i % 2 == 1:
                extra.pop(0)()
        to(H)
        while extra:
            extra.pop(0)()

    loads[0].wait()
    loads[1].wait()
    loads[2].start()
    loads[3].start()
    pl.semaphore_wait(barrier, len(peers))

    def state_chunk(h):
        ks, vs = parts(k[:, cols(h)]), parts(v[:, cols(h)])
        new = [tn(kk * lmb[...], vv).astype(BF16) for kk, vv in zip(ks, vs)]
        for u in range(PAIR):
            st[0, h + u] = new[u]

    def state_other(i, x):
        state_chunk(other + i * CHUNK)
        state_copy(0, (1 - core) * C + i).start()
        return x

    def state_mine(i, x):
        state_chunk(mine + i * CHUNK)
        begin_step(0, fwd, i)
        state_copy(0, core * C + i).start()
        return x

    lax.fori_loop(0, C, state_other, 0)
    lax.fori_loop(0, C, state_mine, 0)
    loads[2].wait()

    def local_forward(h):
        qs_, ks_, vs_ = parts(q[:, cols(h)]), parts(k[:, cols(h)]), parts(v[:, cols(h)])
        top = [(nt(a[:T2], b[:T2]) * mask[:T2, :T2]).astype(BF16) for a, b in zip(qs_, ks_)]
        low = [(nt(a[T2:], b) * mask[T2:, :]).astype(BF16) for a, b in zip(qs_, ks_)]
        up = [nn(a, b[:T2]) for a, b in zip(top, vs_)]
        down = [nn(a, b) for a, b in zip(low, vs_)]
        for u in range(PAIR):
            scr[h + u, :T2, :T2] = top[u]
            scr[h + u, T2:, :] = low[u]
        att[:T2, cols(h)] = joined(up)
        att[T2:, cols(h)] = joined(down)

    loads[3].wait()
    acc[...] = jnp.zeros_like(acc)

    def finish_forward(h, pre):
        carry = [
            (f_state * sr[0, h + u].astype(F32) + f_pre * pre[u].astype(F32)).astype(BF16)
            for u in range(PAIR)
        ]
        old, up = parts(att[:, cols(h)]), parts(g[:, cols(h)])
        query = parts(q[:, cols(h)])
        gains = [gain_ref[pl.ds(h + u, 1), :] for u in range(PAIR)]
        x = [old[u] + fmf[...] * nn(query[u], carry[u]) for u in range(PAIR)]
        squares = sum(x[u] * x[u] for u in range(PAIR))
        inners = sum((up[u].astype(F32) * gains[u]) * x[u] for u in range(PAIR))
        acc[0] += squares
        acc[1] += inners
        for u in range(PAIR):
            ci[h + u] = carry[u]
        att[:, cols(h)] = joined(x)

    def forward_mine(c):
        finish_forward(mine + c * PAIR, [pf[0, c * PAIR + u] for u in range(PAIR)])

    interleave(
        0, fwd, lambda i: local_forward(lax.rem(mine + i, H)), 0, [], forward_mine
    )

    def forward_other(c, x):
        state_copy(0, (1 - core) * C + c).wait_recv()
        final_copy(0, c).wait_recv()
        finish_forward(other + c * PAIR, [pr[0, c * PAIR + u] for u in range(PAIR)])
        return x

    lax.fori_loop(0, C, forward_other, 0)

    squares = jnp.sum(acc[0].T, axis=0, keepdims=True)
    inners = jnp.sum(acc[1].T, axis=0, keepdims=True)
    which = lax.broadcasted_iota(jnp.int32, (8, T), 0)
    sums = jnp.where(which < 4, squares, inners)
    for j, peer in enumerate(tensor_peers):
        ts[j] = sums
        swap = remote(ts.at[j], tr.at[j], tensor_base + j, peer)
        swap.start()
        swap.wait()
        sums = sums + tr[j]
    width = W * n_tensor
    rscale = lax.rsqrt(sums[0:1] / width + EPSILON)
    inner = rscale * sums[4:5] / width
    rs[...] = jnp.broadcast_to(rscale, (HD, T)).T
    qs[...] = jnp.broadcast_to(rscale * rscale * inner, (HD, T)).T

    def back_chunk(h):
        old = parts(att[:, cols(h)])
        ups = [p.astype(F32) for p in parts(g[:, cols(h)])]
        query = parts(q[:, cols(h)])
        gains = [gain_ref[pl.ds(h + u, 1), :] for u in range(PAIR)]
        unit = [old[u] * rs[...] for u in range(PAIR)]
        out = [(gains[u] * unit[u]).astype(BF16) for u in range(PAIR)]
        gsum = [jnp.sum(ups[u] * unit[u], axis=0, keepdims=True) for u in range(PAIR)]
        d = [
            (rs[...] * (ups[u] * gains[u]) - qs[...] * old[u]).astype(BF16)
            for u in range(PAIR)
        ]
        new = [tn(query[u] * fmb[...], d[u]).astype(BF16) for u in range(PAIR)]
        lo[:, cols(h)] = joined(out)
        dat[:, cols(h)] = joined(d)
        for u in range(PAIR):
            gs[0, pl.ds(h + u, 1), :] = gsum[u]
            st[1, h + u] = new[u]

    def back_other(i, x):
        back_chunk(other + i * CHUNK)
        state_copy(1, (1 - core) * C + i).start()
        return x

    def back_mine(i, x):
        back_chunk(mine + i * CHUNK)
        begin_step(1, bwd, i)
        state_copy(1, core * C + i).start()
        return x

    lax.fori_loop(0, C, back_other, 0)
    lax.fori_loop(0, C, back_mine, 0)
    out_lo = pltpu.make_async_copy(lo, lo_hbm, out_sem.at[3 * H])
    out_lo.start()

    gain_peers = dp_peers + seq_peers[::-1]

    def gain_copy(j):
        return remote(gs.at[j], gr.at[j], gain_base + j, gain_peers[j])

    gain_copy(0).start()

    def gain_step(j):
        gain_copy(j).wait_recv()
        total = gs[j] + gr[j]
        if j + 1 < len(gain_peers):
            gs[j + 1] = total
            gain_copy(j + 1).start()
        else:
            gg_ref[...] = total

    def out_copy(n, src, dst, h):
        return pltpu.make_async_copy(src.at[:, cols(h)], dst.at[:, cols(h)], out_sem.at[n * H + h])

    def local_backward(h):
        qs_, ks_, vs_ = parts(q[:, cols(h)]), parts(k[:, cols(h)]), parts(v[:, cols(h)])
        ds_ = parts(dat[:, cols(h)])
        two = range(PAIR)
        stop = [scr[h + u, :T2, :T2] for u in two]
        slow = [scr[h + u, T2:, :] for u in two]
        carry = [ci[h + u] for u in two]
        top = [(nt(ds_[u][:T2], vs_[u][:T2]) * mask[:T2, :T2]).astype(BF16) for u in two]
        low = [(nt(ds_[u][T2:], vs_[u]) * mask[T2:, :]).astype(BF16) for u in two]
        v_up = [tn(stop[u], ds_[u][:T2]) + tn(slow[u][:, :T2], ds_[u][T2:]) for u in two]
        v_down = [tn(slow[u][:, T2:], ds_[u][T2:]) for u in two]
        into = [nt(ds_[u], carry[u]) * fmf[...] for u in two]
        q_up = [nn(top[u], ks_[u][:T2]) + into[u][:T2] for u in two]
        q_down = [nn(low[u], ks_[u]) + into[u][T2:] for u in two]
        k_up = [tn(top[u], qs_[u][:T2]) + tn(low[u][:, :T2], qs_[u][T2:]) for u in two]
        k_down = [tn(low[u][:, T2:], qs_[u][T2:]) for u in two]
        gv[:T2, cols(h)] = joined(v_up).astype(BF16)
        gv[T2:, cols(h)] = joined(v_down).astype(BF16)
        gq[:T2, cols(h)] = joined(q_up).astype(BF16)
        gq[T2:, cols(h)] = joined(q_down).astype(BF16)
        gk[:T2, cols(h)] = joined(k_up).astype(BF16)
        gk[T2:, cols(h)] = joined(k_down).astype(BF16)
        out_copy(0, gq, gq_hbm, h).start()
        out_copy(1, gk, gk_hbm, h).start()
        out_copy(2, gv, gv_hbm, h).start()

    interleave(
        1, bwd, local_backward, 0,
        [functools.partial(gain_step, j) for j in range(len(gain_peers))],
    )

    def finish_backward(h, pre):
        carry = [
            (b_state * sr[1, h + u].astype(F32) + b_pre * pre[u].astype(F32)).astype(BF16)
            for u in range(PAIR)
        ]
        for u in range(PAIR):
            cb[h + u] = carry[u]

    def backward_mine(i, x):
        finish_backward(mine + i * PAIR, [pf[1, i * PAIR + u] for u in range(PAIR)])
        return x

    lax.fori_loop(0, half // PAIR, backward_mine, 0)

    def backward_other(c, x):
        state_copy(1, (1 - core) * C + c).wait_recv()
        final_copy(1, c).wait_recv()
        finish_backward(other + c * PAIR, [pr[1, c * PAIR + u] for u in range(PAIR)])
        return x

    lax.fori_loop(0, C, backward_other, 0)

    for w in range(2):
        def drain(c, x, w=w):
            state_copy(w, c).wait_send()
            state_copy(w, C + c).wait_send()
            for j in range(J):
                step_copy(w, j, c).wait_send()
            final_copy(w, c).wait_send()
            return x

        lax.fori_loop(0, C, drain, 0)
    for j in range(len(gain_peers)):
        gain_copy(j).wait_send()
    out_lo.wait()

    def drain_out(i, x):
        h = i * PAIR
        out_copy(0, gq, gq_hbm, h).wait()
        out_copy(1, gk, gk_hbm, h).wait()
        out_copy(2, gv, gv_hbm, h).wait()
        return x

    lax.fori_loop(0, H // PAIR, drain_out, 0)


def finish_kernel(lo_in, gq_in, gk_in, gv_in, k, v, cb, lm, gg_in, lo, gq, gk, gv, gg):
    lo[...] = lo_in[...]
    gq[...] = gq_in[...]
    gg[...] = gg_in[...]
    for h in range(k.shape[1] // HD):
        here = slice(h * HD, (h + 1) * HD)
        more_k = lm[...] * nt(v[:, here], cb[h])
        more_v = lm[...] * nn(k[:, here], cb[h])
        gk[:, here] = (gk_in[:, here].astype(F32) + more_k).astype(BF16)
        gv[:, here] = (gv_in[:, here].astype(F32) + more_v).astype(BF16)


def body(sizes, queries, keys, values, grad_out, doc_lengths, gain):
    n_dp, n_seq, n_tensor = sizes
    _, T, W = queries.shape
    H = W // HD
    half = H // 2
    C = half // CHUNK
    J = bits_of(n_seq) - 1
    docs = doc_lengths.shape[1]
    per = (3 + J) * C
    n_gain = bits_of(n_dp) + bits_of(n_seq)
    n_copy = 2 * per + bits_of(n_tensor) + n_gain
    big = jax.ShapeDtypeStruct((T, W), BF16)
    anywhere = pl.BlockSpec(memory_space=pl.ANY)
    vmem = pl.BlockSpec(memory_space=pltpu.VMEM)
    wide = pltpu.VMEM((T, W), BF16)
    wide32 = pltpu.VMEM((T, W), F32)
    args = (queries[0], keys[0], values[0], grad_out[0], gain.reshape(H, HD))
    sums = jax.ShapeDtypeStruct((H, HD), F32)
    carries = jax.ShapeDtypeStruct((H, HD, HD), BF16)
    rows = jax.ShapeDtypeStruct((T, HD), F32)
    column = pltpu.VMEM((T, HD), F32)
    column16 = pltpu.VMEM((T, HD), BF16)
    outs = pl.pallas_call(
        functools.partial(kernel, (n_dp, n_seq, n_tensor, docs)),
        out_shape=(big, big, big, big, sums, carries, rows),
        in_specs=[pl.BlockSpec(memory_space=pltpu.SMEM)] + [anywhere] * 4 + [vmem],
        out_specs=[anywhere] * 4 + [vmem] * 3,
        scratch_shapes=[
            wide, wide, wide, wide,
            wide32,
            pltpu.VMEM((H, T, T), BF16),
            wide, wide, wide, wide, wide,
            pltpu.VMEM((T, T), F32),
            column, column16, column16,
            pltpu.VMEM((2, T, HD), F32),
            column, column,
            pltpu.VMEM((2, H, HD, HD), BF16),
            pltpu.VMEM((2, H, HD, HD), BF16),
            pltpu.VMEM((2, J, half, HD, HD), BF16),
            pltpu.VMEM((2, J, half, HD, HD), BF16),
            pltpu.VMEM((half, HD, HD), F32),
            pltpu.VMEM((2, half, HD, HD), BF16),
            pltpu.VMEM((2, half, HD, HD), BF16),
            pltpu.VMEM((H, HD, HD), BF16),
            pltpu.VMEM((bits_of(n_tensor), 8, T), F32),
            pltpu.VMEM((bits_of(n_tensor), 8, T), F32),
            pltpu.VMEM((n_gain, H, HD), F32),
            pltpu.VMEM((n_gain, H, HD), F32),
            pltpu.SemaphoreType.DMA((4,)),
            pltpu.SemaphoreType.DMA((3 * H + 1,)),
            pltpu.SemaphoreType.DMA((n_copy,)),
            pltpu.SemaphoreType.DMA((n_copy,)),
        ],
        compiler_params=pltpu.CompilerParams(
            collective_id=0, has_side_effects=True, vmem_limit_bytes=43 * 1024 * 1024
        ),
        cost_estimate=pl.CostEstimate(
            flops=16 * T * T * W, bytes_accessed=16 * T * W, transcendentals=0
        ),
    )(doc_lengths, *args)
    lo, gq, gk, gv, gg, cb, lm = outs
    step_rows = min(T, 128)
    block = pl.BlockSpec((step_rows, W), lambda i: (i, 0))
    whole = pl.BlockSpec((H, HD), lambda i: (0, 0))
    lo, gq, gk, gv, gg = pl.pallas_call(
        finish_kernel,
        grid=(T // step_rows,),
        out_shape=(big, big, big, big, sums),
        in_specs=[block] * 6 + [
            pl.BlockSpec((H, HD, HD), lambda i: (0, 0, 0)),
            pl.BlockSpec((step_rows, HD), lambda i: (i, 0)),
            whole,
        ],
        out_specs=[block] * 4 + [whole],
        compiler_params=pltpu.CompilerParams(vmem_limit_bytes=14 * 1024 * 1024),
        cost_estimate=pl.CostEstimate(
            flops=4 * T * W * HD, bytes_accessed=20 * T * W, transcendentals=0
        ),
    )(lo, gq, gk, gv, keys[0], values[0], cb, lm, gg)
    return lo[None], gq[None], gk[None], gv[None], gg.reshape(W)


def solution(mesh):
    big = P("dp", "seq", "tensor")
    sizes = tuple(mesh.shape[axis] for axis in ("dp", "seq", "tensor"))
    return jax.shard_map(
        functools.partial(body, sizes),
        mesh=mesh,
        in_specs=(big, big, big, big, P("dp", None), P("tensor")),
        out_specs=(big, big, big, big, P("tensor")),
        check_vma=False,
    )
```
